32 devices in a mesh: inst: 4 (over y, x), page: 4 (over z), head: 2 (over core).
Axes of the slice: x: 2, y: 2, z: 4, core: 2. Of those that a mesh axis runs over, the one named last changes fastest.
Arguments:
- queries: bfloat16 [8, 8192], P('inst', 'head'), may hold values from -21 to 21
- fresh_key_value: bfloat16 [2, 8, 1024], P(None, 'inst', 'head'), may hold values from -8 to 8
- key_value_pool: bfloat16 [2, 2048, 16, 1024], P(None, ('inst', 'page'), None, 'head'), may hold values from -21 to 21
- block_table: int32 [8, 384], P('inst'), may hold values from -1 to 2047, as said below
- lengths: int32 [8], P('inst'), may hold values from 17 to 6144, as said below
Outputs:
- attn: bfloat16 [8, 8192], P('inst', 'head')
The draws below stay inside these ranges and needn't reach their ends.
Inputs may be any that keep to these rules, and one draw needn't show every extreme that they name: `block_table`: request r is owned by instance r // 2. Entries 0 to ceil(lengths[r] / 16) - 1 of row r are pool page numbers below 2048, distinct over all requests; every other entry is -1. `lengths`: every request has two or more pages; some request has exactly 384 full pages.
All inputs are finite; a program needn't handle non-finite values.
Results may differ from the reference program's by a relative error of at most 0.001.
Values may be sent and summed in bfloat16 or wider, within the bound.
A program may use at most 192 MiB of HBM per device.

```python
import math
import jax
import jax.numpy as jnp
from jax import lax

QUERY_HEADS = 64
KEY_VALUE_HEADS = 8
HEAD_SIZE = 128
PAGE_TOKENS = 16
REQUEST_COUNT = 8
POOL_PAGES = 2048
REQUEST_PAGES = 384


def draw_plan(key):
    plan_key = jax.random.fold_in(key, 11)
    count_key = jax.random.fold_in(plan_key, 1)
    pick_key = jax.random.fold_in(plan_key, 2)
    fill_key = jax.random.fold_in(plan_key, 3)
    shuffle_key = jax.random.fold_in(plan_key, 4)
    request_ids = jnp.arange(REQUEST_COUNT, dtype=jnp.int32)
    page_count = jax.random.randint(count_key, (REQUEST_COUNT,), REQUEST_PAGES // 4, REQUEST_PAGES // 2 + 1)
    longest = jax.random.randint(pick_key, (), 0, REQUEST_COUNT)
    page_count = jnp.where(request_ids == longest, REQUEST_PAGES, page_count)
    last_fill = jax.random.randint(fill_key, (REQUEST_COUNT,), 1, PAGE_TOKENS + 1)
    last_fill = jnp.where(request_ids == longest, PAGE_TOKENS, last_fill)
    token_count = (page_count - 1) * PAGE_TOKENS + last_fill
    shuffled = jax.random.permutation(shuffle_key, POOL_PAGES).astype(jnp.int32)
    first_slot = jnp.cumsum(page_count) - page_count
    column = jnp.arange(REQUEST_PAGES, dtype=jnp.int32)
    position = jnp.minimum(first_slot[:, None] + column[None, :], POOL_PAGES - 1)
    page_table = jnp.where(column[None, :] < page_count[:, None], shuffled[position], -1)
    return (token_count.astype(jnp.int32), page_table.astype(jnp.int32))


def query_outputs(key):
    query_key = jax.random.fold_in(key, 23)
    return jnp.clip(3.0 * jax.random.normal(query_key, (REQUEST_COUNT, QUERY_HEADS, HEAD_SIZE), jnp.float32), -18.0, 18.0)


def draw_lengths(key, part):
    token_count, _ = draw_plan(key)
    return token_count


def draw_block_table(key, part):
    _, page_table = draw_plan(key)
    return page_table


def draw_queries(key, part):
    return query_outputs(key).reshape(REQUEST_COUNT, QUERY_HEADS * HEAD_SIZE).astype(jnp.bfloat16)


def draw_key_value_pool(key, part):
    pool_key = jax.random.fold_in(key, 37)
    pool_dimensions = (2, POOL_PAGES, PAGE_TOKENS, KEY_VALUE_HEADS * HEAD_SIZE)
    value_rows = jnp.clip(jax.random.normal(pool_key, pool_dimensions, jnp.float32), -6.0, 6.0)
    return value_rows.astype(jnp.bfloat16)


def level_of(key, dims, pieces, least, top_value):
    def one(dim, blocks):
        steps = jax.random.uniform(jax.random.fold_in(jax.random.fold_in(key, 6), dim), (blocks,), jnp.float32, least / len(pieces), top_value / len(pieces))
        return jnp.repeat(jnp.exp(steps), dims[dim] // blocks).reshape((-1,) + (1,) * (len(dims) - dim - 1))

    factor_of = one(*pieces[0])
    for cut in pieces[1:]:
        factor_of = factor_of * one(*cut)
    return factor_of


def centred(own_key, dims, scale, limit, cuts=(), kind=jnp.bfloat16):
    values = scale * jax.random.normal(own_key, dims, jnp.float32)
    if cuts:
        values = values * level_of(own_key, dims, cuts, -0.22, 0.18)
    return jnp.clip(values, -limit, limit).astype(kind)


def setup_inputs(seed: int = 0) -> dict:
    splits = jax.random.split(jax.random.key(seed), 6)
    queries = draw_queries(jax.random.fold_in(splits[5], 71), 0)
    fresh_key_value = centred(splits[1], (2, REQUEST_COUNT, KEY_VALUE_HEADS * HEAD_SIZE), 2.0, 8.0, ((1, 4), (2, 2)))
    key_value_pool = draw_key_value_pool(jax.random.fold_in(splits[5], 71), 0)
    block_table = draw_block_table(jax.random.fold_in(splits[5], 71), 0)
    lengths = draw_lengths(jax.random.fold_in(splits[5], 71), 0)
    return dict(queries=queries, fresh_key_value=fresh_key_value, key_value_pool=key_value_pool, block_table=block_table, lengths=lengths)


LOWEST_SCORE = -1e+30

def reference(queries, fresh_key_value, key_value_pool, block_table, lengths):
    inverse_sqrt_scale = 1.0 / math.sqrt(HEAD_SIZE)
    columns = jnp.arange(REQUEST_PAGES, dtype=jnp.int32)
    offsets = jnp.arange(PAGE_TOKENS, dtype=jnp.int32)

    def one_request(inputs):
        single_query, fresh_key, fresh_value, table_row, length = inputs
        live_page = columns * PAGE_TOKENS < length
        page_indices = jnp.where(live_page, table_row, 0).astype(jnp.int32)
        paged_keys = key_value_pool[0, page_indices].astype(jnp.float32).reshape(REQUEST_PAGES, PAGE_TOKENS, KEY_VALUE_HEADS, HEAD_SIZE)
        paged_values = key_value_pool[1, page_indices].astype(jnp.float32).reshape(REQUEST_PAGES, PAGE_TOKENS, KEY_VALUE_HEADS, HEAD_SIZE)
        grouped_queries = single_query.astype(jnp.float32).reshape(KEY_VALUE_HEADS, QUERY_HEADS // KEY_VALUE_HEADS, HEAD_SIZE)
        scores = jnp.einsum('gqd,stgd->sgqt', grouped_queries, paged_keys) * inverse_sqrt_scale
        valid = columns[:, None] * PAGE_TOKENS + offsets[None, :] < length
        valid = valid[:, None, None, :]
        masked = jnp.where(valid, scores, LOWEST_SCORE)
        page_max = lax.optimization_barrier(jnp.max(masked, axis=3))
        raw_weight = jnp.where(valid, jnp.exp(masked - page_max[..., None]), 0.0)
        page_sum = lax.optimization_barrier(jnp.sum(raw_weight, axis=3))
        rounded = lax.optimization_barrier(raw_weight.astype(jnp.bfloat16))
        page_out = jnp.einsum('sgqt,stgd->sgqd', rounded.astype(jnp.float32), paged_values)
        fresh_score = jnp.einsum('sxh,sh->sx', grouped_queries, fresh_key.astype(jnp.float32).reshape(KEY_VALUE_HEADS, HEAD_SIZE)) * inverse_sqrt_scale
        top_score = jnp.maximum(lax.optimization_barrier(jnp.max(page_max, axis=0)), fresh_score)
        factor = jnp.exp(page_max - top_score[None])
        own_weight = jnp.exp(fresh_score - top_score)
        denominator = own_weight + lax.optimization_barrier(jnp.sum(factor * page_sum, axis=0))
        self_value = fresh_value.astype(jnp.float32).reshape(KEY_VALUE_HEADS, 1, HEAD_SIZE)
        weighted = own_weight[..., None] * self_value + lax.optimization_barrier(jnp.sum(factor[..., None] * page_out, axis=0))
        return (weighted / denominator[..., None]).reshape(QUERY_HEADS * HEAD_SIZE).astype(jnp.bfloat16)
    return lax.map(one_request, (queries, fresh_key_value[0], fresh_key_value[1], block_table, lengths))
```

```python
import functools
import math

import jax
import jax.numpy as jnp
from jax import lax
from jax.experimental import pallas as pl
from jax.experimental.pallas import tpu as pltpu
from jax.sharding import PartitionSpec as P

HEAD_SIZE = 128
LOWEST_SCORE = -1e30
SCALE = 1.0 / math.sqrt(HEAD_SIZE)
CHUNK_SLOTS = 16
MESH = pl.DeviceIdType.MESH


def kernel(
    insts, pages, groups,
    q_ref, fresh_ref, len_ref, table_ref, pool_ref, out_ref,
    keys, values, values_t, q_own, q_all, t_own, t_all, raw, page_max, weights, send, recv,
    fresh_score, fresh_value,
    pool_sem, q_send, q_recv, t_send, t_recv, x_send, x_recv, o_send, o_recv,
):
    own = q_ref.shape[0]
    heads = q_ref.shape[1] // HEAD_SIZE
    per_group = heads // groups
    pairs = groups // 2
    requests = own * insts
    columns = table_ref.shape[1]
    slots, page_tok = keys.shape[0], keys.shape[1]
    tokens = slots * page_tok
    width = requests * per_group
    lanes = 2 * width
    stat_rows = pairs * lanes // 128
    devices = insts * pages
    units = own * groups // pages
    unit_rows = units * per_group

    me_i = lax.axis_index("inst")
    me_p = lax.axis_index("page")
    me = me_i * pages + me_p

    key_copy = pltpu.make_async_copy(pool_ref.at[0], keys, pool_sem.at[0])
    value_copy = pltpu.make_async_copy(pool_ref.at[1], values, pool_sem.at[1])
    value_copy.start()
    key_copy.start()

    barrier = pltpu.get_barrier_semaphore()

    def greet(k, carry):
        other = lax.rem(me + k, devices)
        pl.semaphore_signal(
            barrier, inc=1,
            device_id={"inst": lax.div(other, pages), "page": lax.rem(other, pages)},
            device_id_type=MESH,
        )
        return carry

    lax.fori_loop(1, devices, greet, 0)

    q = q_ref[...].astype(jnp.float32)
    fresh = fresh_ref[...].astype(jnp.float32)
    grouped = []
    for g in range(groups):
        rows = jnp.concatenate(
            [
                q[r : r + 1, (g * per_group + h) * HEAD_SIZE : (g * per_group + h + 1) * HEAD_SIZE]
                for r in range(own)
                for h in range(per_group)
            ],
            axis=0,
        )
        grouped.append(rows)
        q_own[g] = rows.astype(jnp.bfloat16)
    column = lax.broadcasted_iota(jnp.int32, (own, columns), 1)
    row = lax.broadcasted_iota(jnp.int32, (own, columns), 0)
    length = jnp.zeros((own, columns), jnp.int32)
    for r in range(own):
        length = jnp.where(row == r, len_ref[r], length)
    fill = jnp.clip(length - column * page_tok, 0, page_tok)
    t_own[...] = jnp.where(fill > 0, table_ref[...] * 32 + fill, -1)

    pl.semaphore_wait(barrier, devices - 1)

    def gather_copies(k):
        to = {"inst": lax.rem(me_i + k, insts)}
        return (
            pltpu.make_async_remote_copy(
                src_ref=q_own, dst_ref=q_all.at[me_i], send_sem=q_send.at[k],
                recv_sem=q_recv.at[k], device_id=to, device_id_type=MESH,
            ),
            pltpu.make_async_remote_copy(
                src_ref=t_own, dst_ref=t_all.at[me_i], send_sem=t_send.at[k],
                recv_sem=t_recv.at[k], device_id=to, device_id_type=MESH,
            ),
        )

    for k in range(1, insts):
        for copy in gather_copies(k):
            copy.start()
    q_all[me_i] = q_own[...]
    t_all[me_i] = t_own[...]

    for unit in range(own * groups):
        r, g = unit // groups, unit % groups
        p, u = unit // units, unit % units
        cut = slice(g * HEAD_SIZE, (g + 1) * HEAD_SIZE)
        products = grouped[g][r * per_group : (r + 1) * per_group] * fresh[0, r : r + 1, cut]
        score = jnp.sum(products, axis=1, keepdims=True) * SCALE
        place = slice(u * per_group, (u + 1) * per_group)
        fresh_score[p, place] = jnp.broadcast_to(score, (per_group, HEAD_SIZE))
        fresh_value[p, place] = jnp.broadcast_to(fresh[1, r : r + 1, cut], (per_group, HEAD_SIZE))

    value_copy.wait()
    for pair in range(pairs):
        cut = slice(pair * 2 * HEAD_SIZE, (pair + 1) * 2 * HEAD_SIZE)
        values_t[pair] = values[:, :, cut].reshape(tokens, 2 * HEAD_SIZE).T

    key_copy.wait()
    for k in range(1, insts):
        for copy in gather_copies(k):
            copy.wait()

    first = me * slots
    slot_id = lax.broadcasted_iota(jnp.int32, (slots, columns), 0) + first
    lane_request = lax.rem(lax.broadcasted_iota(jnp.int32, (slots, lanes), 1), width) // per_group
    filled = jnp.zeros((slots, lanes), jnp.int32)
    for i in range(insts):
        packed = t_all[i]
        page_id = packed >> 5
        page_fill = packed & 31
        for r in range(own):
            hit = jnp.where(slot_id == page_id[r : r + 1], page_fill[r : r + 1], 0)
            count = jnp.sum(hit.astype(jnp.float32), axis=1, keepdims=True).astype(jnp.int32)
            filled = jnp.where(lane_request == i * own + r, count, filled)

    pair_queries = []
    for pair in range(pairs):
        low = q_all[:, 2 * pair].reshape(width, HEAD_SIZE)
        high = q_all[:, 2 * pair + 1].reshape(width, HEAD_SIZE)
        none = jnp.zeros_like(low)
        pair_queries.append(
            jnp.concatenate(
                [jnp.concatenate([low, none], axis=1), jnp.concatenate([none, high], axis=1)], axis=0
            )
        )

    offset = lax.broadcasted_iota(jnp.int32, (CHUNK_SLOTS, page_tok, lanes), 1)
    chunk_tokens = CHUNK_SLOTS * page_tok
    for c in range(slots // CHUNK_SLOTS):
        here = slice(c * CHUNK_SLOTS, (c + 1) * CHUNK_SLOTS)
        valid = offset < filled[here][:, None, :]
        for pair in range(pairs):
            cut = slice(pair * 2 * HEAD_SIZE, (pair + 1) * 2 * HEAD_SIZE)
            scores = lax.dot_general(
                keys[here, :, cut].reshape(chunk_tokens, 2 * HEAD_SIZE),
                pair_queries[pair],
                (((1,), (1,)), ((), ())),
                preferred_element_type=jnp.float32,
            ).reshape(CHUNK_SLOTS, page_tok, lanes) * SCALE
            masked = jnp.where(valid, scores, LOWEST_SCORE)
            top = jnp.max(masked, axis=1)
            page_max[pair, here] = top
            raw[pair, here] = jnp.exp(masked - top[:, None, :])

    stats = []
    parts = []
    for pair in range(pairs):
        tops = page_max[pair]
        local_max = jnp.max(tops, axis=0, keepdims=True)
        factor = jnp.where(filled > 0, jnp.exp(tops - local_max), 0.0)
        total = jnp.zeros((page_tok, lanes), jnp.float32)
        for c in range(slots // CHUNK_SLOTS):
            here = slice(c * CHUNK_SLOTS, (c + 1) * CHUNK_SLOTS)
            scale = factor[here][:, None, :]
            weight = raw[pair, here]
            total += jnp.sum(weight * scale, axis=0)
            scaled = weight.astype(jnp.bfloat16).astype(jnp.float32) * scale
            upper = scaled.astype(jnp.bfloat16)
            lower = (scaled - upper.astype(jnp.float32)).astype(jnp.bfloat16)
            rows = slice(c * chunk_tokens, (c + 1) * chunk_tokens)
            weights[pair, rows, :lanes] = upper.reshape(chunk_tokens, lanes)
            weights[pair, rows, lanes:] = lower.reshape(chunk_tokens, lanes)
        stats.append((local_max, jnp.sum(total, axis=0, keepdims=True)))
        both = jnp.dot(values_t[pair], weights[pair], preferred_element_type=jnp.float32)
        both = both[:, :lanes] + both[:, lanes:]
        lane = lax.broadcasted_iota(jnp.int32, (HEAD_SIZE, lanes), 1)
        parts.append(jnp.where(lane < width, both[:HEAD_SIZE], both[HEAD_SIZE:]).T)

    stat_block = jnp.concatenate(
        [
            stats[pair][kind][:, b * 128 : (b + 1) * 128]
            for kind in range(2)
            for pair in range(pairs)
            for b in range(lanes // 128)
        ],
        axis=0,
    )
    for i in range(insts):
        for unit in range(own * groups):
            r, g = unit // groups, unit % groups
            p, u = unit // units, unit % units
            start = (g % 2) * width + (i * own + r) * per_group
            send[i * pages + p, u * per_group : (u + 1) * per_group] = parts[g // 2][
                start : start + per_group
            ]
        for p in range(pages):
            send[i * pages + p, unit_rows : unit_rows + 2 * stat_rows] = stat_block

    def exchange(k):
        other = lax.rem(me + k, devices)
        return pltpu.make_async_remote_copy(
            src_ref=send.at[other], dst_ref=recv.at[me], send_sem=x_send.at[k],
            recv_sem=x_recv.at[k],
            device_id={"inst": lax.div(other, pages), "page": lax.rem(other, pages)},
            device_id_type=MESH,
        )

    def start_exchange(k, carry):
        exchange(k).start()
        return carry

    def wait_exchange(k, carry):
        exchange(k).wait()
        return carry

    lax.fori_loop(1, devices, start_exchange, 0)
    recv[me] = send[me]
    lax.fori_loop(1, devices, wait_exchange, 0)

    row = lax.broadcasted_iota(jnp.int32, (1, unit_rows, 128), 1)
    lane = lax.broadcasted_iota(jnp.int32, (1, unit_rows, 128), 2)
    unit = me_p * units + row // per_group
    r, g = unit // groups, lax.rem(unit, groups)
    place = (
        (g // 2) * lanes + lax.rem(g, 2) * width
        + (me_i * own + r) * per_group + lax.rem(row, per_group)
    )
    picked = []
    for kind in range(2):
        found = jnp.zeros((devices, unit_rows, 128), jnp.float32)
        for b in range(stat_rows):
            at = unit_rows + kind * stat_rows + b
            found = jnp.where(place == b * 128 + lane, recv[:, at : at + 1, :], found)
        picked.append(jnp.sum(found, axis=2, keepdims=True))
    maxima, totals = picked
    own_score = fresh_score[me_p]
    top = jnp.maximum(jnp.max(maxima, axis=0), own_score)
    carried = jnp.exp(maxima - top[None])
    own_weight = jnp.exp(own_score - top)
    denominator = own_weight + jnp.sum(carried * totals, axis=0)
    numerator = own_weight * fresh_value[me_p] + jnp.sum(carried * recv[:, :unit_rows, :], axis=0)
    out_ref[me_p] = (numerator / denominator).astype(out_ref.dtype)

    def result_copy(k):
        return pltpu.make_async_remote_copy(
            src_ref=out_ref.at[me_p], dst_ref=out_ref.at[me_p], send_sem=o_send.at[k],
            recv_sem=o_recv.at[k], device_id={"page": lax.rem(me_p + k, pages)},
            device_id_type=MESH,
        )

    for k in range(1, pages):
        result_copy(k).start()
    for k in range(1, pages):
        result_copy(k).wait()


def shards(insts, pages, queries, fresh_key_value, key_value_pool, block_table, lengths):
    own = queries.shape[0]
    slots, page_tok, depth = key_value_pool.shape[1:]
    groups = depth // HEAD_SIZE
    heads = queries.shape[1] // HEAD_SIZE
    per_group = heads // groups
    pairs = groups // 2
    columns = block_table.shape[1]
    lanes = 2 * own * insts * per_group
    stat_rows = pairs * lanes // 128
    devices = insts * pages
    unit_rows = own * heads // pages
    block_rows = unit_rows + (2 * stat_rows + 7) // 8 * 8
    vmem = pl.BlockSpec(memory_space=pltpu.VMEM)
    dma = pltpu.SemaphoreType.DMA
    out = pl.pallas_call(
        functools.partial(kernel, insts, pages, groups),
        out_shape=jax.ShapeDtypeStruct((pages, unit_rows, HEAD_SIZE), jnp.bfloat16),
        in_specs=[
            vmem, vmem, pl.BlockSpec(memory_space=pltpu.SMEM), vmem,
            pl.BlockSpec(memory_space=pl.ANY),
        ],
        out_specs=vmem,
        scratch_shapes=[
            pltpu.VMEM((slots, page_tok, depth), jnp.bfloat16),
            pltpu.VMEM((slots, page_tok, depth), jnp.bfloat16),
            pltpu.VMEM((pairs, 2 * HEAD_SIZE, slots * page_tok), jnp.bfloat16),
            pltpu.VMEM((groups, own * per_group, HEAD_SIZE), jnp.bfloat16),
            pltpu.VMEM((insts, groups, own * per_group, HEAD_SIZE), jnp.bfloat16),
            pltpu.VMEM((own, columns), jnp.int32),
            pltpu.VMEM((insts, own, columns), jnp.int32),
            pltpu.VMEM((pairs, slots, page_tok, lanes), jnp.float32),
            pltpu.VMEM((pairs, slots, lanes), jnp.float32),
            pltpu.VMEM((pairs, slots * page_tok, 2 * lanes), jnp.bfloat16),
            pltpu.VMEM((devices, block_rows, 128), jnp.float32),
            pltpu.VMEM((devices, block_rows, 128), jnp.float32),
            pltpu.VMEM((pages, unit_rows, HEAD_SIZE), jnp.float32),
            pltpu.VMEM((pages, unit_rows, HEAD_SIZE), jnp.float32),
            dma((2,)),
            dma((insts,)), dma((insts,)), dma((insts,)), dma((insts,)),
            dma((devices,)), dma((devices,)),
            dma((pages,)), dma((pages,)),
        ],
        compiler_params=pltpu.CompilerParams(
            collective_id=0, has_side_effects=True, vmem_limit_bytes=56 * 1024 * 1024
        ),
        cost_estimate=pl.CostEstimate(
            flops=8 * slots * page_tok * lanes * HEAD_SIZE * pairs,
            bytes_accessed=4 * slots * page_tok * depth,
            transcendentals=slots * page_tok * lanes * pairs,
        ),
        name="paged_attention",
    )(queries, fresh_key_value, lengths, block_table, key_value_pool)
    return out.reshape(own, heads * HEAD_SIZE)


def solution(mesh):
    return jax.shard_map(
        functools.partial(shards, mesh.shape["inst"], mesh.shape["page"]),
        mesh=mesh,
        in_specs=(
            P("inst", "head"),
            P(None, "inst", "head"),
            P(None, ("inst", "page"), None, "head"),
            P("inst", None),
            P("inst"),
        ),
        out_specs=P("inst", "head"),
        check_vma=False,
    )
```

```python
import functools
import math

import jax
import jax.numpy as jnp
from jax import lax
from jax.experimental import pallas as pl
from jax.experimental.pallas import tpu as pltpu
from jax.sharding import PartitionSpec as P

HEAD_SIZE = 128
LOWEST_SCORE = -1e30
EXPONENT = math.log2(math.e) / math.sqrt(HEAD_SIZE)
CHUNK_SLOTS = 16
MESH = pl.DeviceIdType.MESH


def slot_of(pages, p):
    return p + p // 2 - 2 * (p // 3) if pages == 4 else p


def kernel(
    insts, pages, groups,
    q_hbm, fresh_hbm, len_hbm, table_hbm, pool_hbm, out_hbm,
    q_ref, fresh_ref, len_ref, table_ref,
    keys, values, values_t, q_own, q_all, t_own, t_all, raw, page_max, weights, send, recv,
    fresh_score, fresh_value, result,
    in_sem, pool_sem, q_send, q_recv, t_send, t_recv, x_send, x_recv, o_send, o_recv, o_own,
):
    own = q_ref.shape[0]
    heads = q_ref.shape[1] // HEAD_SIZE
    per_group = heads // groups
    pairs = groups // 2
    requests = own * insts
    columns = table_ref.shape[1]
    slots, page_tok = keys.shape[0], keys.shape[1]
    tokens = slots * page_tok
    width = requests * per_group
    lanes = 2 * width
    stat_rows = lanes // 128
    devices = insts * pages
    units = own * groups // pages
    unit_rows = units * per_group

    me_i = lax.axis_index("inst")
    me_p = lax.axis_index("page")
    me = me_i * pages + me_p
    me_slot = slot_of(pages, me_p)

    barrier = pltpu.get_barrier_semaphore()

    def greet(k, carry):
        other = lax.rem(me + k, devices)
        pl.semaphore_signal(
            barrier, inc=1,
            device_id={"inst": lax.div(other, pages), "page": lax.rem(other, pages)},
            device_id_type=MESH,
        )
        return carry

    lax.fori_loop(1, devices, greet, 0)

    small = [
        pltpu.make_async_copy(source, target, in_sem.at[k])
        for k, (source, target) in enumerate(
            [(q_hbm, q_ref), (len_hbm, len_ref), (table_hbm, table_ref), (fresh_hbm, fresh_ref)]
        )
    ]
    for copy in small:
        copy.start()
    value_copy = pltpu.make_async_copy(pool_hbm.at[1], values, pool_sem.at[1])
    key_copy = pltpu.make_async_copy(pool_hbm.at[0], keys, pool_sem.at[0])
    value_copy.start()
    key_copy.start()
    for copy in small:
        copy.wait()

    q = q_ref[...].astype(jnp.float32)
    fresh = fresh_ref[...].astype(jnp.float32)
    grouped = []
    for g in range(groups):
        rows = jnp.concatenate(
            [
                q[r : r + 1, (g * per_group + h) * HEAD_SIZE : (g * per_group + h + 1) * HEAD_SIZE]
                for r in range(own)
                for h in range(per_group)
            ],
            axis=0,
        )
        grouped.append(rows)
        q_own[g] = rows.astype(jnp.bfloat16)
    column = lax.broadcasted_iota(jnp.int32, (own, columns), 1)
    row = lax.broadcasted_iota(jnp.int32, (own, columns), 0)
    length = jnp.zeros((own, columns), jnp.int32)
    for r in range(own):
        length = jnp.where(row == r, len_ref[r], length)
    fill = jnp.clip(length - column * page_tok, 0, page_tok)
    t_own[...] = jnp.where(
        fill > 0, table_ref[...] * 1024 + (me_i * own + row) * 32 + fill, -1
    )

    pl.semaphore_wait(barrier, devices - 1)

    def gather_copies(k):
        to = {"inst": lax.rem(me_i + k, insts)}
        return (
            pltpu.make_async_remote_copy(
                src_ref=q_own, dst_ref=q_all.at[me_i], send_sem=q_send.at[k],
                recv_sem=q_recv.at[k], device_id=to, device_id_type=MESH,
            ),
            pltpu.make_async_remote_copy(
                src_ref=t_own, dst_ref=t_all.at[me_i], send_sem=t_send.at[k],
                recv_sem=t_recv.at[k], device_id=to, device_id_type=MESH,
            ),
        )

    for k in range(1, insts):
        for copy in gather_copies(k):
            copy.start()
    q_all[me_i] = q_own[...]
    t_all[me_i] = t_own[...]

    for unit in range(own * groups):
        r, g = unit // groups, unit % groups
        slot, u = unit // units, unit % units
        cut = slice(g * HEAD_SIZE, (g + 1) * HEAD_SIZE)
        products = grouped[g][r * per_group : (r + 1) * per_group] * fresh[0, r : r + 1, cut]
        score = jnp.sum(products, axis=1, keepdims=True)
        place = slice(u * per_group, (u + 1) * per_group)
        fresh_score[slot, place] = jnp.broadcast_to(score, (per_group, HEAD_SIZE))
        fresh_value[slot, place] = jnp.broadcast_to(fresh[1, r : r + 1, cut], (per_group, HEAD_SIZE))

    value_copy.wait()
    for pair in range(pairs):
        cut = slice(pair * 2 * HEAD_SIZE, (pair + 1) * 2 * HEAD_SIZE)
        values_t[pair] = values[:, :, cut].reshape(tokens, 2 * HEAD_SIZE).T

    key_copy.wait()
    for k in range(1, insts):
        for copy in gather_copies(k):
            copy.wait()

    slot_id = lax.broadcasted_iota(jnp.int32, (slots, 128), 0) + me * slots
    code = jnp.zeros((slots, 128), jnp.int32)
    for i in range(insts):
        packed = t_all[i]
        page_id = packed >> 10
        page_code = packed & 1023
        for r in range(own):
            for b in range(0, columns, 128):
                code += jnp.where(
                    slot_id == page_id[r : r + 1, b : b + 128], page_code[r : r + 1, b : b + 128], 0
                )
    code = jnp.sum(code.astype(jnp.float32), axis=1, keepdims=True).astype(jnp.int32)
    lane_request = lax.rem(lax.broadcasted_iota(jnp.int32, (slots, lanes), 1), width) // per_group
    filled = jnp.where(lane_request == code >> 5, code & 31, 0)

    offset = lax.broadcasted_iota(jnp.int32, (CHUNK_SLOTS, page_tok, lanes), 1)
    lane = lax.broadcasted_iota(jnp.int32, (HEAD_SIZE, lanes), 1)
    chunk_tokens = CHUNK_SLOTS * page_tok
    chunks = [slice(c * CHUNK_SLOTS, (c + 1) * CHUNK_SLOTS) for c in range(slots // CHUNK_SLOTS)]

    def exchange(to_i, to_p):
        to = to_i * pages + to_p
        return pltpu.make_async_remote_copy(
            src_ref=send.at[to], dst_ref=recv.at[me], send_sem=x_send.at[to],
            recv_sem=x_recv.at[me], device_id={"inst": to_i, "page": to_p}, device_id_type=MESH,
        )

    for pair in range(pairs):
        cut = slice(pair * 2 * HEAD_SIZE, (pair + 1) * 2 * HEAD_SIZE)
        low = q_all[:, 2 * pair].reshape(width, HEAD_SIZE)
        high = q_all[:, 2 * pair + 1].reshape(width, HEAD_SIZE)
        none = jnp.zeros_like(low)
        pair_queries = jnp.concatenate(
            [jnp.concatenate([low, none], axis=1), jnp.concatenate([none, high], axis=1)], axis=0
        )
        for here in chunks:
            scores = lax.dot_general(
                keys[here, :, cut].reshape(chunk_tokens, 2 * HEAD_SIZE),
                pair_queries,
                (((1,), (1,)), ((), ())),
                preferred_element_type=jnp.float32,
            ).reshape(CHUNK_SLOTS, page_tok, lanes)
            masked = jnp.where(offset < filled[here][:, None, :], scores, LOWEST_SCORE)
            top = jnp.max(masked, axis=1)
            page_max[pair, here] = top
            raw[pair, here] = jnp.exp2((masked - top[:, None, :]) * EXPONENT)
        tops = page_max[pair]
        local_max = jnp.max(tops, axis=0, keepdims=True)
        factor = jnp.where(filled > 0, jnp.exp2((tops - local_max) * EXPONENT), 0.0)
        total = jnp.zeros((page_tok, lanes), jnp.float32)
        for c, here in enumerate(chunks):
            scale = factor[here][:, None, :]
            weight = raw[pair, here]
            total += jnp.sum(weight * scale, axis=0)
            scaled = weight.astype(jnp.bfloat16).astype(jnp.float32) * scale
            upper = scaled.astype(jnp.bfloat16)
            lower = (scaled - upper.astype(jnp.float32)).astype(jnp.bfloat16)
            rows = slice(c * chunk_tokens, (c + 1) * chunk_tokens)
            weights[pair, rows, :lanes] = upper.reshape(chunk_tokens, lanes)
            weights[pair, rows, lanes:] = lower.reshape(chunk_tokens, lanes)
        total = jnp.sum(total, axis=0, keepdims=True)
        both = jnp.dot(values_t[pair], weights[pair], preferred_element_type=jnp.float32)
        both = both[:, :lanes] + both[:, lanes:]
        part = jnp.where(lane < width, both[:HEAD_SIZE], both[HEAD_SIZE:]).T
        stats = jnp.concatenate(
            [x[:, b * 128 : (b + 1) * 128] for x in (local_max, total) for b in range(stat_rows)],
            axis=0,
        )
        targets = [
            p for p in range(pages) if slot_of(pages, p) * units % groups // 2 == pair
        ]
        for p in targets:
            for i in range(insts):
                send[i * pages + p, unit_rows:] = stats
                for u in range(units):
                    r, g = divmod(slot_of(pages, p) * units + u, groups)
                    start = (g % 2) * width + (i * own + r) * per_group
                    send[i * pages + p, u * per_group : (u + 1) * per_group] = part[
                        start : start + per_group
                    ]

        def start_exchange(k, carry):
            for p in targets:
                exchange(lax.rem(me_i + k, insts), p).start()
            return carry

        lax.fori_loop(1, insts, start_exchange, 0)
        for p in targets:
            @pl.when(me_p != p)
            def _():
                exchange(me_i, p).start()

    recv[me] = send[me]

    def wait_exchange(k, carry):
        other = lax.rem(me + k, devices)
        pltpu.make_async_remote_copy(
            src_ref=send.at[other], dst_ref=recv.at[other], send_sem=x_send.at[other],
            recv_sem=x_recv.at[other],
            device_id={"inst": lax.div(other, pages), "page": lax.rem(other, pages)},
            device_id_type=MESH,
        ).wait()
        return carry

    lax.fori_loop(1, devices, wait_exchange, 0)

    row = lax.broadcasted_iota(jnp.int32, (1, unit_rows, 128), 1)
    lane = lax.broadcasted_iota(jnp.int32, (1, unit_rows, 128), 2)
    unit = me_slot * units + row // per_group
    r, g = unit // groups, lax.rem(unit, groups)
    place = lax.rem(g, 2) * width + (me_i * own + r) * per_group + lax.rem(row, per_group)
    picked = []
    for kind in range(2):
        found = jnp.zeros((devices, unit_rows, 128), jnp.float32)
        for b in range(stat_rows):
            at = unit_rows + kind * stat_rows + b
            found = jnp.where(place == b * 128 + lane, recv[:, at : at + 1, :], found)
        picked.append(jnp.sum(found, axis=2, keepdims=True))
    maxima, totals = picked
    own_score = fresh_score[me_slot]
    top = jnp.maximum(jnp.max(maxima, axis=0), own_score)
    carried = jnp.exp2((maxima - top[None]) * EXPONENT)
    own_weight = jnp.exp2((own_score - top) * EXPONENT)
    denominator = own_weight + jnp.sum(carried * totals, axis=0)
    numerator = own_weight * fresh_value[me_slot] + jnp.sum(
        carried * recv[:, :unit_rows, :], axis=0
    )
    result[...] = (numerator / denominator).astype(result.dtype)

    def result_copy(k):
        return pltpu.make_async_remote_copy(
            src_ref=result, dst_ref=out_hbm.at[me_slot], send_sem=o_send.at[k],
            recv_sem=o_recv.at[k], device_id={"page": lax.rem(me_p + k, pages)},
            device_id_type=MESH,
        )

    for k in range(1, pages):
        result_copy(k).start()
    own_copy = pltpu.make_async_copy(result, out_hbm.at[me_slot], o_own)
    own_copy.start()
    own_copy.wait()
    for k in range(1, pages):
        result_copy(k).wait()


def shards(insts, pages, queries, fresh_key_value, key_value_pool, block_table, lengths):
    own = queries.shape[0]
    slots, page_tok, depth = key_value_pool.shape[1:]
    groups = depth // HEAD_SIZE
    heads = queries.shape[1] // HEAD_SIZE
    per_group = heads // groups
    pairs = groups // 2
    columns = block_table.shape[1]
    lanes = 2 * own * insts * per_group
    devices = insts * pages
    unit_rows = own * heads // pages
    block_rows = unit_rows + 2 * lanes // 128
    hbm = pl.BlockSpec(memory_space=pl.ANY)
    dma = pltpu.SemaphoreType.DMA
    out = pl.pallas_call(
        functools.partial(kernel, insts, pages, groups),
        out_shape=jax.ShapeDtypeStruct((pages, unit_rows, HEAD_SIZE), jnp.bfloat16),
        in_specs=[hbm] * 5,
        out_specs=hbm,
        scratch_shapes=[
            pltpu.VMEM(queries.shape, jnp.bfloat16),
            pltpu.VMEM(fresh_key_value.shape, jnp.bfloat16),
            pltpu.SMEM(lengths.shape, jnp.int32),
            pltpu.VMEM(block_table.shape, jnp.int32),
            pltpu.VMEM((slots, page_tok, depth), jnp.bfloat16),
            pltpu.VMEM((slots, page_tok, depth), jnp.bfloat16),
            pltpu.VMEM((pairs, 2 * HEAD_SIZE, slots * page_tok), jnp.bfloat16),
            pltpu.VMEM((groups, own * per_group, HEAD_SIZE), jnp.bfloat16),
            pltpu.VMEM((insts, groups, own * per_group, HEAD_SIZE), jnp.bfloat16),
            pltpu.VMEM((own, columns), jnp.int32),
            pltpu.VMEM((insts, own, columns), jnp.int32),
            pltpu.VMEM((pairs, slots, page_tok, lanes), jnp.float32),
            pltpu.VMEM((pairs, slots, lanes), jnp.float32),
            pltpu.VMEM((pairs, slots * page_tok, 2 * lanes), jnp.bfloat16),
            pltpu.VMEM((devices, block_rows, 128), jnp.float32),
            pltpu.VMEM((devices, block_rows, 128), jnp.float32),
            pltpu.VMEM((pages, unit_rows, HEAD_SIZE), jnp.float32),
            pltpu.VMEM((pages, unit_rows, HEAD_SIZE), jnp.float32),
            pltpu.VMEM((unit_rows, HEAD_SIZE), jnp.bfloat16),
            dma((4,)), dma((2,)),
            dma((insts,)), dma((insts,)), dma((insts,)), dma((insts,)),
            dma((devices,)), dma((devices,)),
            dma((pages,)), dma((pages,)), dma(()),
        ],
        compiler_params=pltpu.CompilerParams(
            collective_id=0, has_side_effects=True, vmem_limit_bytes=56 * 1024 * 1024
        ),
        cost_estimate=pl.CostEstimate(
            flops=8 * slots * page_tok * lanes * HEAD_SIZE * pairs,
            bytes_accessed=4 * slots * page_tok * depth,
            transcendentals=slots * page_tok * lanes * pairs,
        ),
        name="paged_attention",
    )(queries, fresh_key_value, lengths, block_table, key_value_pool)
    return out.reshape(own, heads * HEAD_SIZE)


def solution(mesh):
    return jax.shard_map(
        functools.partial(shards, mesh.shape["inst"], mesh.shape["page"]),
        mesh=mesh,
        in_specs=(
            P("inst", "head"),
            P(None, "inst", "head"),
            P(None, ("inst", "page"), None, "head"),
            P("inst", None),
            P("inst"),
        ),
        out_specs=P("inst", "head"),
        check_vma=False,
    )
```

```python
import functools
import math

import jax
import jax.numpy as jnp
from jax import lax
from jax.experimental import pallas as pl
from jax.experimental.pallas import tpu as pltpu
from jax.sharding import PartitionSpec as P

HEAD_SIZE = 128
LOWEST_SCORE = -1e30
EXPONENT = math.log2(math.e) / math.sqrt(HEAD_SIZE)
BLOCK_ROWS = 16
MESH = pl.DeviceIdType.MESH


def slot_of(pages, p):
    return p + p // 2 - 2 * (p // 3) if pages == 4 else p


def kernel(
    insts, pages, groups,
    q_hbm, fresh_hbm, len_hbm, table_hbm, pool_hbm, out_hbm,
    q_ref, fresh_ref, len_ref, table_ref,
    keys, values, keys_by_token, values_by_token, q_own, q_all, t_own, t_all,
    scores, weights, send, recv,
    columns_of, fresh_score, fresh_value, result,
    in_sem, pool_sem, q_send, q_recv, t_send, t_recv, x_send, x_recv, o_send, o_recv, o_own,
):
    own = q_ref.shape[0]
    heads = q_ref.shape[1] // HEAD_SIZE
    per_group = heads // groups
    pairs = groups // 2
    requests = own * insts
    columns = table_ref.shape[1]
    slots, page_tok = keys.shape[0], keys.shape[1]
    tokens = slots * page_tok
    width = requests * per_group
    lanes = 2 * width
    stat_rows = lanes // 128
    devices = insts * pages
    units = own * groups // pages
    unit_rows = units * per_group

    me_i = lax.axis_index("inst")
    me_p = lax.axis_index("page")
    me = me_i * pages + me_p
    me_slot = slot_of(pages, me_p)

    barrier = pltpu.get_barrier_semaphore()

    def greet(k, carry):
        other = lax.rem(me + k, devices)
        pl.semaphore_signal(
            barrier, inc=1,
            device_id={"inst": lax.div(other, pages), "page": lax.rem(other, pages)},
            device_id_type=MESH,
        )
        return carry

    lax.fori_loop(1, devices, greet, 0)

    small = [
        pltpu.make_async_copy(source, target, in_sem.at[k])
        for k, (source, target) in enumerate(
            [(q_hbm, q_ref), (len_hbm, len_ref), (table_hbm, table_ref), (fresh_hbm, fresh_ref)]
        )
    ]
    for copy in small:
        copy.start()
    value_copy = pltpu.make_async_copy(pool_hbm.at[1], values, pool_sem.at[1])
    key_copy = pltpu.make_async_copy(pool_hbm.at[0], keys, pool_sem.at[0])
    key_copy.start()
    value_copy.start()
    for copy in small:
        copy.wait()

    q = q_ref[...].astype(jnp.float32)
    fresh = fresh_ref[...].astype(jnp.float32)
    grouped = []
    for g in range(groups):
        rows = jnp.concatenate(
            [
                q[r : r + 1, (g * per_group + h) * HEAD_SIZE : (g * per_group + h + 1) * HEAD_SIZE]
                for r in range(own)
                for h in range(per_group)
            ],
            axis=0,
        )
        grouped.append(rows)
        q_own[g] = rows.astype(jnp.bfloat16)
    column = lax.broadcasted_iota(jnp.int32, (own, columns), 1)
    row = lax.broadcasted_iota(jnp.int32, (own, columns), 0)
    length = jnp.zeros((own, columns), jnp.int32)
    for r in range(own):
        length = jnp.where(row == r, len_ref[r], length)
    fill = jnp.clip(length - column * page_tok, 0, page_tok)
    t_own[...] = jnp.where(
        fill > 0, table_ref[...] * 1024 + (me_i * own + row) * 32 + fill, -1
    )

    pl.semaphore_wait(barrier, devices - 1)

    def gather_copies(k):
        to = {"inst": lax.rem(me_i + k, insts)}
        return (
            pltpu.make_async_remote_copy(
                src_ref=q_own, dst_ref=q_all.at[me_i], send_sem=q_send.at[k],
                recv_sem=q_recv.at[k], device_id=to, device_id_type=MESH,
            ),
            pltpu.make_async_remote_copy(
                src_ref=t_own, dst_ref=t_all.at[me_i], send_sem=t_send.at[k],
                recv_sem=t_recv.at[k], device_id=to, device_id_type=MESH,
            ),
        )

    for k in range(1, insts):
        for copy in gather_copies(k):
            copy.start()
    q_all[me_i] = q_own[...]
    t_all[me_i] = t_own[...]

    for unit in range(own * groups):
        r, g = unit // groups, unit % groups
        slot, u = unit // units, unit % units
        cut = slice(g * HEAD_SIZE, (g + 1) * HEAD_SIZE)
        products = grouped[g][r * per_group : (r + 1) * per_group] * fresh[0, r : r + 1, cut]
        score = jnp.sum(products, axis=1, keepdims=True)
        place = slice(u * per_group, (u + 1) * per_group)
        fresh_score[slot, place] = jnp.broadcast_to(score, (per_group, HEAD_SIZE))
        fresh_value[slot, place] = jnp.broadcast_to(fresh[1, r : r + 1, cut], (per_group, HEAD_SIZE))

    chunk = 256 // page_tok
    new = lax.broadcasted_iota(jnp.int32, (256, 256), 0)
    old = lax.broadcasted_iota(jnp.int32, (256, 256), 1)
    moves = (new // chunk == lax.rem(old, page_tok)) & (lax.rem(new, chunk) == old // page_tok)
    moves = jnp.where(moves, 1.0, 0.0).astype(jnp.bfloat16)
    for copy, source, target in (
        (key_copy, keys, keys_by_token), (value_copy, values, values_by_token)
    ):
        copy.wait()
        for c in range(0, slots, chunk):
            moved = jnp.dot(
                moves, source[c : c + chunk].reshape(256, source.shape[2]),
                preferred_element_type=jnp.float32,
            )
            target[:, c : c + chunk, :] = moved.astype(jnp.bfloat16).reshape(
                page_tok, chunk, source.shape[2]
            )

    for k in range(1, insts):
        for copy in gather_copies(k):
            copy.wait()

    slot_id = lax.broadcasted_iota(jnp.int32, (slots, 128), 0) + me * slots
    code = jnp.zeros((slots, 128), jnp.int32)
    for i in range(insts):
        packed = t_all[i]
        page_id = packed >> 10
        page_code = packed & 1023
        for r in range(own):
            for b in range(0, columns, 128):
                code += jnp.where(
                    slot_id == page_id[r : r + 1, b : b + 128], page_code[r : r + 1, b : b + 128], 0
                )
    code = jnp.sum(code.astype(jnp.float32).T, axis=0, keepdims=True).astype(jnp.int32)
    slot_owner = jnp.broadcast_to(code >> 5, (BLOCK_ROWS, slots))
    slot_fill = jnp.broadcast_to(code & 31, (BLOCK_ROWS, slots))
    block_row = lax.broadcasted_iota(jnp.int32, (BLOCK_ROWS, slots), 0)
    lane = lax.broadcasted_iota(jnp.int32, (BLOCK_ROWS, 128), 1)

    def tree(join, items):
        while len(items) > 1:
            items = [join(*items[k : k + 2]) for k in range(0, len(items) - 1, 2)] + (
                items[-1:] if len(items) % 2 else []
            )
        return items[0]

    def exchange(to_i, to_p):
        to = to_i * pages + to_p
        return pltpu.make_async_remote_copy(
            src_ref=send.at[to], dst_ref=recv.at[me], send_sem=x_send.at[to],
            recv_sem=x_recv.at[me], device_id={"inst": to_i, "page": to_p}, device_id_type=MESH,
        )

    for pair in range(pairs):
        cut = slice(pair * 2 * HEAD_SIZE, (pair + 1) * 2 * HEAD_SIZE)
        low = q_all[:, 2 * pair].reshape(width, HEAD_SIZE)
        high = q_all[:, 2 * pair + 1].reshape(width, HEAD_SIZE)
        none = jnp.zeros_like(low)
        pair_queries = jnp.concatenate(
            [jnp.concatenate([low, none], axis=1), jnp.concatenate([none, high], axis=1)], axis=0
        )
        scores[pair] = lax.dot_general(
            pair_queries,
            keys_by_token[:, :, cut].reshape(tokens, 2 * HEAD_SIZE),
            (((1,), (1,)), ((), ())),
            preferred_element_type=jnp.float32,
        )

        def weigh(block, pair=pair):
            first = block * BLOCK_ROWS
            if not isinstance(block, int):
                first = pl.multiple_of(first, BLOCK_ROWS)
            row_request = lax.rem(first + block_row, width) // per_group
            filled = jnp.where(slot_owner == row_request, slot_fill, 0)
            masked = [
                jnp.where(
                    filled > t,
                    scores[pair, pl.ds(first, BLOCK_ROWS), t * slots : (t + 1) * slots],
                    LOWEST_SCORE,
                )
                for t in range(page_tok)
            ]
            page_max = tree(jnp.maximum, masked)
            raw = [jnp.exp2((x - page_max) * EXPONENT) for x in masked]
            page_sum = tree(jnp.add, raw)
            local_max = jnp.max(page_max, axis=1, keepdims=True)
            factor = jnp.where(filled > 0, jnp.exp2((page_max - local_max) * EXPONENT), 0.0)
            total = jnp.sum(page_sum * factor, axis=1, keepdims=True)
            for t in range(page_tok):
                scaled = raw[t].astype(jnp.bfloat16).astype(jnp.float32) * factor
                upper = scaled.astype(jnp.bfloat16)
                lower = (scaled - upper.astype(jnp.float32)).astype(jnp.bfloat16)
                at = slice(t * slots, (t + 1) * slots)
                weights[pair, pl.ds(first, BLOCK_ROWS), at] = upper
                weights[pair, pl.ds(lanes + first, BLOCK_ROWS), at] = lower
            columns_of[pair, pl.ds(first, BLOCK_ROWS)] = jnp.where(lane == 0, local_max, total)

        if lanes <= 128:
            for block in range(lanes // BLOCK_ROWS):
                weigh(block)
        else:
            lax.fori_loop(0, lanes // BLOCK_ROWS, lambda block, carry: (weigh(block), carry)[1], 0)
        both = jnp.dot(
            weights[pair], values_by_token[:, :, cut].reshape(tokens, 2 * HEAD_SIZE),
            preferred_element_type=jnp.float32,
        )
        both = both[:lanes] + both[lanes:]
        part = jnp.concatenate([both[:width, :HEAD_SIZE], both[width:, HEAD_SIZE:]], axis=0)
        stats = columns_of[pair].T
        stats = jnp.concatenate(
            [stats[k : k + 1, b * 128 : (b + 1) * 128] for k in range(2) for b in range(stat_rows)],
            axis=0,
        )
        targets = [
            p for p in range(pages) if slot_of(pages, p) * units % groups // 2 == pair
        ]
        for p in targets:
            for i in range(insts):
                send[i * pages + p, unit_rows:] = stats
                for u in range(units):
                    r, g = divmod(slot_of(pages, p) * units + u, groups)
                    start = (g % 2) * width + (i * own + r) * per_group
                    send[i * pages + p, u * per_group : (u + 1) * per_group] = part[
                        start : start + per_group
                    ]

        def start_exchange(k, carry):
            for p in targets:
                exchange(lax.rem(me_i + k, insts), p).start()
            return carry

        lax.fori_loop(1, insts, start_exchange, 0)
        for p in targets:
            @pl.when(me_p != p)
            def _():
                exchange(me_i, p).start()

    recv[me] = send[me]

    def wait_exchange(k, carry):
        other = lax.rem(me + k, devices)
        pltpu.make_async_remote_copy(
            src_ref=send.at[other], dst_ref=recv.at[other], send_sem=x_send.at[other],
            recv_sem=x_recv.at[other],
            device_id={"inst": lax.div(other, pages), "page": lax.rem(other, pages)},
            device_id_type=MESH,
        ).wait()
        return carry

    lax.fori_loop(1, devices, wait_exchange, 0)

    row = lax.broadcasted_iota(jnp.int32, (1, unit_rows, 128), 1)
    lane = lax.broadcasted_iota(jnp.int32, (1, unit_rows, 128), 2)
    unit = me_slot * units + row // per_group
    r, g = unit // groups, lax.rem(unit, groups)
    place = lax.rem(g, 2) * width + (me_i * own + r) * per_group + lax.rem(row, per_group)
    picked = []
    for kind in range(2):
        found = jnp.zeros((devices, unit_rows, 128), jnp.float32)
        for b in range(stat_rows):
            at = unit_rows + kind * stat_rows + b
            found = jnp.where(place == b * 128 + lane, recv[:, at : at + 1, :], found)
        picked.append(jnp.sum(found, axis=2, keepdims=True))
    maxima, totals = picked
    own_score = fresh_score[me_slot]
    top = jnp.maximum(jnp.max(maxima, axis=0), own_score)
    carried = jnp.exp2((maxima - top[None]) * EXPONENT)
    own_weight = jnp.exp2((own_score - top) * EXPONENT)
    denominator = own_weight + jnp.sum(carried * totals, axis=0)
    numerator = own_weight * fresh_value[me_slot] + jnp.sum(
        carried * recv[:, :unit_rows, :], axis=0
    )
    result[...] = (numerator / denominator).astype(result.dtype)

    def result_copy(k):
        return pltpu.make_async_remote_copy(
            src_ref=result, dst_ref=out_hbm.at[me_slot], send_sem=o_send.at[k],
            recv_sem=o_recv.at[k], device_id={"page": lax.rem(me_p + k, pages)},
            device_id_type=MESH,
        )

    for k in range(1, pages):
        result_copy(k).start()
    own_copy = pltpu.make_async_copy(result, out_hbm.at[me_slot], o_own)
    own_copy.start()
    own_copy.wait()
    for k in range(1, pages):
        result_copy(k).wait()


def shards(insts, pages, queries, fresh_key_value, key_value_pool, block_table, lengths):
    own = queries.shape[0]
    slots, page_tok, depth = key_value_pool.shape[1:]
    groups = depth // HEAD_SIZE
    heads = queries.shape[1] // HEAD_SIZE
    per_group = heads // groups
    pairs = groups // 2
    columns = block_table.shape[1]
    lanes = 2 * own * insts * per_group
    devices = insts * pages
    unit_rows = own * heads // pages
    block_rows = unit_rows + 2 * lanes // 128
    hbm = pl.BlockSpec(memory_space=pl.ANY)
    dma = pltpu.SemaphoreType.DMA
    out = pl.pallas_call(
        functools.partial(kernel, insts, pages, groups),
        out_shape=jax.ShapeDtypeStruct((pages, unit_rows, HEAD_SIZE), jnp.bfloat16),
        in_specs=[hbm] * 5,
        out_specs=hbm,
        scratch_shapes=[
            pltpu.VMEM(queries.shape, jnp.bfloat16),
            pltpu.VMEM(fresh_key_value.shape, jnp.bfloat16),
            pltpu.SMEM(lengths.shape, jnp.int32),
            pltpu.VMEM(block_table.shape, jnp.int32),
            pltpu.VMEM((slots, page_tok, depth), jnp.bfloat16),
            pltpu.VMEM((slots, page_tok, depth), jnp.bfloat16),
            pltpu.VMEM((page_tok, slots, depth), jnp.bfloat16),
            pltpu.VMEM((page_tok, slots, depth), jnp.bfloat16),
            pltpu.VMEM((groups, own * per_group, HEAD_SIZE), jnp.bfloat16),
            pltpu.VMEM((insts, groups, own * per_group, HEAD_SIZE), jnp.bfloat16),
            pltpu.VMEM((own, columns), jnp.int32),
            pltpu.VMEM((insts, own, columns), jnp.int32),
            pltpu.VMEM((pairs, lanes, slots * page_tok), jnp.float32),
            pltpu.VMEM((pairs, 2 * lanes, slots * page_tok), jnp.bfloat16),
            pltpu.VMEM((devices, block_rows, 128), jnp.float32),
            pltpu.VMEM((devices, block_rows, 128), jnp.float32),
            pltpu.VMEM((pairs, lanes, 128), jnp.float32),
            pltpu.VMEM((pages, unit_rows, HEAD_SIZE), jnp.float32),
            pltpu.VMEM((pages, unit_rows, HEAD_SIZE), jnp.float32),
            pltpu.VMEM((unit_rows, HEAD_SIZE), jnp.bfloat16),
            dma((4,)), dma((2,)),
            dma((insts,)), dma((insts,)), dma((insts,)), dma((insts,)),
            dma((devices,)), dma((devices,)),
            dma((pages,)), dma((pages,)), dma(()),
        ],
        compiler_params=pltpu.CompilerParams(
            collective_id=0, has_side_effects=True, vmem_limit_bytes=56 * 1024 * 1024
        ),
        cost_estimate=pl.CostEstimate(
            flops=8 * slots * page_tok * lanes * HEAD_SIZE * pairs,
            bytes_accessed=4 * slots * page_tok * depth,
            transcendentals=slots * page_tok * lanes * pairs,
        ),
        name="paged_attention",
    )(queries, fresh_key_value, lengths, block_table, key_value_pool)
    return out.reshape(own, heads * HEAD_SIZE)


def solution(mesh):
    return jax.shard_map(
        functools.partial(shards, mesh.shape["inst"], mesh.shape["page"]),
        mesh=mesh,
        in_specs=(
            P("inst", "head"),
            P(None, "inst", "head"),
            P(None, ("inst", "page"), None, "head"),
            P("inst", None),
            P("inst"),
        ),
        out_specs=P("inst", "head"),
        check_vma=False,
    )
```

```python
import functools
import math

import jax
import jax.numpy as jnp
from jax import lax
from jax.experimental import pallas as pl
from jax.experimental.pallas import tpu as pltpu
from jax.sharding import PartitionSpec as P

HEAD_SIZE = 128
LOWEST_SCORE = -1e30
EXPONENT = math.log2(math.e) / math.sqrt(HEAD_SIZE)
BLOCK_ROWS = 16
MESH = pl.DeviceIdType.MESH


def slot_of(pages, p):
    return p + p // 2 - 2 * (p // 3) if pages == 4 else p


def kernel(
    insts, pages, groups,
    q_hbm, fresh_hbm, len_hbm, table_hbm, pool_hbm, out_hbm,
    q_ref, fresh_ref, len_ref, table_ref,
    keys, values, keys_by_token, values_by_token, q_own, q_all, t_own, t_all,
    scores, weights, send, recv,
    page_max, page_sum, factors, fresh_score, fresh_value, result,
    in_sem, pool_sem, q_send, q_recv, t_send, t_recv, x_send, x_recv, o_send, o_recv, o_own,
):
    own = q_ref.shape[0]
    heads = q_ref.shape[1] // HEAD_SIZE
    per_group = heads // groups
    pairs = groups // 2
    requests = own * insts
    columns = table_ref.shape[1]
    slots, page_tok = keys.shape[0], keys.shape[1]
    tokens = slots * page_tok
    width = requests * per_group
    lanes = 2 * width
    stat_rows = lanes // 128
    devices = insts * pages
    units = own * groups // pages
    unit_rows = units * per_group

    me_i = lax.axis_index("inst")
    me_p = lax.axis_index("page")
    me = me_i * pages + me_p
    me_slot = slot_of(pages, me_p)

    barrier = pltpu.get_barrier_semaphore()

    def greet(k, carry):
        other = lax.rem(me + k, devices)
        pl.semaphore_signal(
            barrier, inc=1,
            device_id={"inst": lax.div(other, pages), "page": lax.rem(other, pages)},
            device_id_type=MESH,
        )
        return carry

    lax.fori_loop(1, devices, greet, 0)

    small = [
        pltpu.make_async_copy(source, target, in_sem.at[k])
        for k, (source, target) in enumerate(
            [(q_hbm, q_ref), (len_hbm, len_ref), (table_hbm, table_ref), (fresh_hbm, fresh_ref)]
        )
    ]
    for copy in small:
        copy.start()
    value_copy = pltpu.make_async_copy(pool_hbm.at[1], values, pool_sem.at[1])
    key_copy = pltpu.make_async_copy(pool_hbm.at[0], keys, pool_sem.at[0])
    key_copy.start()
    value_copy.start()
    for copy in small:
        copy.wait()

    q = q_ref[...].astype(jnp.float32)
    fresh = fresh_ref[...].astype(jnp.float32)
    grouped = []
    for g in range(groups):
        rows = jnp.concatenate(
            [
                q[r : r + 1, (g * per_group + h) * HEAD_SIZE : (g * per_group + h + 1) * HEAD_SIZE]
                for r in range(own)
                for h in range(per_group)
            ],
            axis=0,
        )
        grouped.append(rows)
        q_own[g] = rows.astype(jnp.bfloat16)
    column = lax.broadcasted_iota(jnp.int32, (own, columns), 1)
    row = lax.broadcasted_iota(jnp.int32, (own, columns), 0)
    length = jnp.zeros((own, columns), jnp.int32)
    for r in range(own):
        length = jnp.where(row == r, len_ref[r], length)
    fill = jnp.clip(length - column * page_tok, 0, page_tok)
    t_own[...] = jnp.where(
        fill > 0, table_ref[...] * 1024 + (me_i * own + row) * 32 + fill, -1
    )

    pl.semaphore_wait(barrier, devices - 1)

    def gather_copies(k):
        to = {"inst": lax.rem(me_i + k, insts)}
        return (
            pltpu.make_async_remote_copy(
                src_ref=q_own, dst_ref=q_all.at[me_i], send_sem=q_send.at[k],
                recv_sem=q_recv.at[k], device_id=to, device_id_type=MESH,
            ),
            pltpu.make_async_remote_copy(
                src_ref=t_own, dst_ref=t_all.at[me_i], send_sem=t_send.at[k],
                recv_sem=t_recv.at[k], device_id=to, device_id_type=MESH,
            ),
        )

    for k in range(1, insts):
        for copy in gather_copies(k):
            copy.start()
    q_all[me_i] = q_own[...]
    t_all[me_i] = t_own[...]

    for unit in range(own * groups):
        r, g = unit // groups, unit % groups
        slot, u = unit // units, unit % units
        cut = slice(g * HEAD_SIZE, (g + 1) * HEAD_SIZE)
        products = grouped[g][r * per_group : (r + 1) * per_group] * fresh[0, r : r + 1, cut]
        score = jnp.sum(products, axis=1, keepdims=True)
        place = slice(u * per_group, (u + 1) * per_group)
        fresh_score[slot, place] = jnp.broadcast_to(score, (per_group, HEAD_SIZE))
        fresh_value[slot, place] = jnp.broadcast_to(fresh[1, r : r + 1, cut], (per_group, HEAD_SIZE))

    chunk = 256 // page_tok
    new = lax.broadcasted_iota(jnp.int32, (256, 256), 0)
    old = lax.broadcasted_iota(jnp.int32, (256, 256), 1)
    moves = (new // chunk == lax.rem(old, page_tok)) & (lax.rem(new, chunk) == old // page_tok)
    moves = jnp.where(moves, 1.0, 0.0).astype(jnp.bfloat16)
    for copy, source, target in (
        (key_copy, keys, keys_by_token), (value_copy, values, values_by_token)
    ):
        copy.wait()

        def move(step, carry, source=source, target=target):
            for half in range(2):
                c = pl.multiple_of((2 * step + half) * chunk, chunk)
                moved = jnp.dot(
                    moves, source[pl.ds(c, chunk)].reshape(256, source.shape[2]),
                    preferred_element_type=jnp.float32,
                )
                target[:, pl.ds(c, chunk), :] = moved.astype(jnp.bfloat16).reshape(
                    page_tok, chunk, source.shape[2]
                )
            return carry

        lax.fori_loop(0, slots // chunk // 2, move, 0)

    for k in range(1, insts):
        for copy in gather_copies(k):
            copy.wait()

    slot_id = lax.broadcasted_iota(jnp.int32, (slots, 128), 0) + me * slots

    def match(i, code):
        packed = t_all[i]
        page_id = packed >> 10
        page_code = packed & 1023
        for r in range(own):
            for b in range(0, columns, 128):
                code += jnp.where(
                    slot_id == page_id[r : r + 1, b : b + 128], page_code[r : r + 1, b : b + 128], 0
                )
        return code

    code = lax.fori_loop(0, insts, match, jnp.zeros((slots, 128), jnp.int32))
    code = jnp.sum(code.astype(jnp.float32).T, axis=0, keepdims=True).astype(jnp.int32)
    code = jnp.where(code == 0, requests * 32, code)
    slot_owner = jnp.broadcast_to(code >> 5, (BLOCK_ROWS, slots))
    slot_fill = jnp.broadcast_to(code & 31, (BLOCK_ROWS, slots))
    block_row = lax.broadcasted_iota(jnp.int32, (BLOCK_ROWS, slots), 0)
    lane = lax.broadcasted_iota(jnp.int32, (lanes, 128), 1)

    def tree(join, items):
        while len(items) > 1:
            items = [join(*items[k : k + 2]) for k in range(0, len(items) - 1, 2)] + (
                items[-1:] if len(items) % 2 else []
            )
        return items[0]

    def exchange(to_i, to_p):
        to = to_i * pages + to_p
        return pltpu.make_async_remote_copy(
            src_ref=send.at[to], dst_ref=recv.at[me], send_sem=x_send.at[to],
            recv_sem=x_recv.at[me], device_id={"inst": to_i, "page": to_p}, device_id_type=MESH,
        )

    for pair in range(pairs):
        cut = slice(pair * 2 * HEAD_SIZE, (pair + 1) * 2 * HEAD_SIZE)
        low = q_all[:, 2 * pair].reshape(width, HEAD_SIZE)
        high = q_all[:, 2 * pair + 1].reshape(width, HEAD_SIZE)
        none = jnp.zeros_like(low)
        pair_queries = jnp.concatenate(
            [jnp.concatenate([low, none], axis=1), jnp.concatenate([none, high], axis=1)], axis=0
        )
        scores[pair] = lax.dot_general(
            pair_queries,
            keys_by_token[:, :, cut].reshape(tokens, 2 * HEAD_SIZE),
            (((1,), (1,)), ((), ())),
            preferred_element_type=jnp.float32,
        )

        def owned_tokens(first):
            row_request = lax.rem(first + block_row, width) // per_group
            return jnp.where(slot_owner == row_request, slot_fill, 0)

        def masked_scores(first, filled, pair=pair):
            return [
                jnp.where(
                    filled > t,
                    scores[pair, pl.ds(first, BLOCK_ROWS), t * slots : (t + 1) * slots],
                    LOWEST_SCORE,
                )
                for t in range(page_tok)
            ]

        def maximum(block, carry):
            first = pl.multiple_of(block * BLOCK_ROWS, BLOCK_ROWS)
            page_max[pl.ds(first, BLOCK_ROWS)] = tree(
                jnp.maximum, masked_scores(first, owned_tokens(first))
            )
            return carry

        def weigh(block, carry, pair=pair):
            first = pl.multiple_of(block * BLOCK_ROWS, BLOCK_ROWS)
            filled = owned_tokens(first)
            tops = page_max[pl.ds(first, BLOCK_ROWS)]
            factor = factors[pl.ds(first, BLOCK_ROWS)]
            raw = [
                jnp.exp2((x - tops) * EXPONENT) for x in masked_scores(first, filled)
            ]
            page_sum[pl.ds(first, BLOCK_ROWS)] = tree(jnp.add, raw) * factor
            for t in range(page_tok):
                scaled = raw[t].astype(jnp.bfloat16).astype(jnp.float32) * factor
                upper = scaled.astype(jnp.bfloat16)
                lower = (scaled - upper.astype(jnp.float32)).astype(jnp.bfloat16)
                at = slice(t * slots, (t + 1) * slots)
                weights[pair, pl.ds(first, BLOCK_ROWS), at] = upper
                weights[pair, pl.ds(lanes + first, BLOCK_ROWS), at] = lower
            return carry

        blocks = lanes // BLOCK_ROWS
        lax.fori_loop(0, blocks, maximum, 0)
        tops = page_max[...]
        local_max = jnp.max(tops, axis=1, keepdims=True)
        all_rows = lax.broadcasted_iota(jnp.int32, (lanes, slots), 0)
        owned = code >> 5 == lax.rem(all_rows, width) // per_group
        factors[...] = jnp.where(owned, jnp.exp2((tops - local_max) * EXPONENT), 0.0)
        lax.fori_loop(0, blocks, weigh, 0)
        total = jnp.sum(page_sum[...], axis=1, keepdims=True)
        columns_of = jnp.where(lane == 0, local_max, total)
        both = jnp.dot(
            weights[pair], values_by_token[:, :, cut].reshape(tokens, 2 * HEAD_SIZE),
            preferred_element_type=jnp.float32,
        )
        both = both[:lanes] + both[lanes:]
        part = jnp.concatenate([both[:width, :HEAD_SIZE], both[width:, HEAD_SIZE:]], axis=0)
        stats = columns_of.T
        stats = jnp.concatenate(
            [stats[k : k + 1, b * 128 : (b + 1) * 128] for k in range(2) for b in range(stat_rows)],
            axis=0,
        )
        targets = [
            p for p in range(pages) if slot_of(pages, p) * units % groups // 2 == pair
        ]
        for p in targets:
            for i in range(insts):
                send[i * pages + p, unit_rows:] = stats
                for u in range(units):
                    r, g = divmod(slot_of(pages, p) * units + u, groups)
                    start = (g % 2) * width + (i * own + r) * per_group
                    send[i * pages + p, u * per_group : (u + 1) * per_group] = part[
                        start : start + per_group
                    ]

        def start_exchange(k, carry):
            for p in targets:
                exchange(lax.rem(me_i + k, insts), p).start()
            return carry

        lax.fori_loop(1, insts, start_exchange, 0)
        for p in targets:
            @pl.when(me_p != p)
            def _():
                exchange(me_i, p).start()

    recv[me] = send[me]

    def wait_exchange(k, carry):
        other = lax.rem(me + k, devices)
        pltpu.make_async_remote_copy(
            src_ref=send.at[other], dst_ref=recv.at[other], send_sem=x_send.at[other],
            recv_sem=x_recv.at[other],
            device_id={"inst": lax.div(other, pages), "page": lax.rem(other, pages)},
            device_id_type=MESH,
        ).wait()
        return carry

    lax.fori_loop(1, devices, wait_exchange, 0)

    row = lax.broadcasted_iota(jnp.int32, (1, unit_rows, 128), 1)
    lane = lax.broadcasted_iota(jnp.int32, (1, unit_rows, 128), 2)
    unit = me_slot * units + row // per_group
    r, g = unit // groups, lax.rem(unit, groups)
    place = lax.rem(g, 2) * width + (me_i * own + r) * per_group + lax.rem(row, per_group)
    picked = []
    for kind in range(2):
        found = jnp.zeros((devices, unit_rows, 128), jnp.float32)
        for b in range(stat_rows):
            at = unit_rows + kind * stat_rows + b
            found = jnp.where(place == b * 128 + lane, recv[:, at : at + 1, :], found)
        picked.append(jnp.sum(found, axis=2, keepdims=True))
    maxima, totals = picked
    own_score = fresh_score[me_slot]
    top = jnp.maximum(jnp.max(maxima, axis=0), own_score)
    carried = jnp.exp2((maxima - top[None]) * EXPONENT)
    own_weight = jnp.exp2((own_score - top) * EXPONENT)
    denominator = own_weight + jnp.sum(carried * totals, axis=0)
    numerator = own_weight * fresh_value[me_slot] + jnp.sum(
        carried * recv[:, :unit_rows, :], axis=0
    )
    result[...] = (numerator / denominator).astype(result.dtype)

    def result_copy(k):
        return pltpu.make_async_remote_copy(
            src_ref=result, dst_ref=out_hbm.at[me_slot], send_sem=o_send.at[k],
            recv_sem=o_recv.at[k], device_id={"page": lax.rem(me_p + k, pages)},
            device_id_type=MESH,
        )

    for k in range(1, pages):
        result_copy(k).start()
    own_copy = pltpu.make_async_copy(result, out_hbm.at[me_slot], o_own)
    own_copy.start()
    own_copy.wait()
    for k in range(1, pages):
        result_copy(k).wait()


def shards(insts, pages, queries, fresh_key_value, key_value_pool, block_table, lengths):
    own = queries.shape[0]
    slots, page_tok, depth = key_value_pool.shape[1:]
    groups = depth // HEAD_SIZE
    heads = queries.shape[1] // HEAD_SIZE
    per_group = heads // groups
    pairs = groups // 2
    columns = block_table.shape[1]
    lanes = 2 * own * insts * per_group
    devices = insts * pages
    unit_rows = own * heads // pages
    block_rows = unit_rows + 2 * lanes // 128
    hbm = pl.BlockSpec(memory_space=pl.ANY)
    dma = pltpu.SemaphoreType.DMA
    out = pl.pallas_call(
        functools.partial(kernel, insts, pages, groups),
        out_shape=jax.ShapeDtypeStruct((pages, unit_rows, HEAD_SIZE), jnp.bfloat16),
        in_specs=[hbm] * 5,
        out_specs=hbm,
        scratch_shapes=[
            pltpu.VMEM(queries.shape, jnp.bfloat16),
            pltpu.VMEM(fresh_key_value.shape, jnp.bfloat16),
            pltpu.SMEM(lengths.shape, jnp.int32),
            pltpu.VMEM(block_table.shape, jnp.int32),
            pltpu.VMEM((slots, page_tok, depth), jnp.bfloat16),
            pltpu.VMEM((slots, page_tok, depth), jnp.bfloat16),
            pltpu.VMEM((page_tok, slots, depth), jnp.bfloat16),
            pltpu.VMEM((page_tok, slots, depth), jnp.bfloat16),
            pltpu.VMEM((groups, own * per_group, HEAD_SIZE), jnp.bfloat16),
            pltpu.VMEM((insts, groups, own * per_group, HEAD_SIZE), jnp.bfloat16),
            pltpu.VMEM((own, columns), jnp.int32),
            pltpu.VMEM((insts, own, columns), jnp.int32),
            pltpu.VMEM((pairs, lanes, slots * page_tok), jnp.float32),
            pltpu.VMEM((pairs, 2 * lanes, slots * page_tok), jnp.bfloat16),
            pltpu.VMEM((devices, block_rows, 128), jnp.float32),
            pltpu.VMEM((devices, block_rows, 128), jnp.float32),
            pltpu.VMEM((lanes, slots), jnp.float32),
            pltpu.VMEM((lanes, slots), jnp.float32),
            pltpu.VMEM((lanes, slots), jnp.float32),
            pltpu.VMEM((pages, unit_rows, HEAD_SIZE), jnp.float32),
            pltpu.VMEM((pages, unit_rows, HEAD_SIZE), jnp.float32),
            pltpu.VMEM((unit_rows, HEAD_SIZE), jnp.bfloat16),
            dma((4,)), dma((2,)),
            dma((insts,)), dma((insts,)), dma((insts,)), dma((insts,)),
            dma((devices,)), dma((devices,)),
            dma((pages,)), dma((pages,)), dma(()),
        ],
        compiler_params=pltpu.CompilerParams(
            collective_id=0, has_side_effects=True, vmem_limit_bytes=56 * 1024 * 1024
        ),
        cost_estimate=pl.CostEstimate(
            flops=8 * slots * page_tok * lanes * HEAD_SIZE * pairs,
            bytes_accessed=4 * slots * page_tok * depth,
            transcendentals=slots * page_tok * lanes * pairs,
        ),
        name="paged_attention",
    )(queries, fresh_key_value, lengths, block_table, key_value_pool)
    return out.reshape(own, heads * HEAD_SIZE)


def solution(mesh):
    return jax.shard_map(
        functools.partial(shards, mesh.shape["inst"], mesh.shape["page"]),
        mesh=mesh,
        in_specs=(
            P("inst", "head"),
            P(None, "inst", "head"),
            P(None, ("inst", "page"), None, "head"),
            P("inst", None),
            P("inst"),
        ),
        out_specs=P("inst", "head"),
        check_vma=False,
    )
```

```python
import functools
import math

import jax
import jax.numpy as jnp
from jax import lax
from jax.experimental import pallas as pl
from jax.experimental.pallas import tpu as pltpu
from jax.sharding import PartitionSpec as P

HEAD_SIZE = 128
LOWEST_SCORE = -1e30
EXPONENT = math.log2(math.e) / math.sqrt(HEAD_SIZE)
BLOCK_ROWS = 16
POOL_PIECES = 4
MESH = pl.DeviceIdType.MESH


def slot_of(pages, p):
    return p + p // 2 - 2 * (p // 3) if pages == 4 else p


def kernel(
    insts, pages, groups,
    q_hbm, fresh_hbm, len_hbm, table_hbm, pool_hbm, out_hbm,
    q_ref, fresh_ref, len_ref, table_ref,
    keys, values, keys_by_token, values_by_token, q_own, q_all, t_own, t_all,
    scores, weights, send, recv,
    columns_of, fresh_score, fresh_value, result,
    in_sem, pool_sem, q_send, q_recv, t_send, t_recv, x_send, x_recv, o_send, o_recv, o_own,
):
    own = q_ref.shape[0]
    heads = q_ref.shape[1] // HEAD_SIZE
    per_group = heads // groups
    pairs = groups // 2
    requests = own * insts
    columns = table_ref.shape[1]
    slots, page_tok = keys.shape[0], keys.shape[1]
    tokens = slots * page_tok
    width = requests * per_group
    lanes = 2 * width
    stat_rows = lanes // 128
    devices = insts * pages
    units = own * groups // pages
    unit_rows = units * per_group

    me_i = lax.axis_index("inst")
    me_p = lax.axis_index("page")
    me = me_i * pages + me_p
    me_slot = slot_of(pages, me_p)

    barrier = pltpu.get_barrier_semaphore()

    def greet(k, carry):
        other = lax.rem(me + k, devices)
        pl.semaphore_signal(
            barrier, inc=1,
            device_id={"inst": lax.div(other, pages), "page": lax.rem(other, pages)},
            device_id_type=MESH,
        )
        return carry

    lax.fori_loop(1, devices, greet, 0)

    small = [
        pltpu.make_async_copy(source, target, in_sem.at[k])
        for k, (source, target) in enumerate(
            [(q_hbm, q_ref), (len_hbm, len_ref), (table_hbm, table_ref), (fresh_hbm, fresh_ref)]
        )
    ]
    for copy in small:
        copy.start()
    piece = slots // POOL_PIECES
    pool_copies = [
        pltpu.make_async_copy(
            pool_hbm.at[kind, pl.ds(c * piece, piece)], target.at[pl.ds(c * piece, piece)],
            pool_sem.at[kind, c],
        )
        for kind, target in enumerate((keys, values))
        for c in range(POOL_PIECES)
    ]
    for copy in pool_copies:
        copy.start()
    for copy in small:
        copy.wait()

    q = q_ref[...].astype(jnp.float32)
    fresh = fresh_ref[...].astype(jnp.float32)
    grouped = []
    for g in range(groups):
        rows = jnp.concatenate(
            [
                q[r : r + 1, (g * per_group + h) * HEAD_SIZE : (g * per_group + h + 1) * HEAD_SIZE]
                for r in range(own)
                for h in range(per_group)
            ],
            axis=0,
        )
        grouped.append(rows)
        q_own[g] = rows.astype(jnp.bfloat16)
    column = lax.broadcasted_iota(jnp.int32, (own, columns), 1)
    row = lax.broadcasted_iota(jnp.int32, (own, columns), 0)
    length = jnp.zeros((own, columns), jnp.int32)
    for r in range(own):
        length = jnp.where(row == r, len_ref[r], length)
    fill = jnp.clip(length - column * page_tok, 0, page_tok)
    t_own[...] = jnp.where(
        fill > 0, table_ref[...] * 1024 + (me_i * own + row) * 32 + fill, -1
    )

    pl.semaphore_wait(barrier, devices - 1)

    def gather_copies(k):
        to = {"inst": lax.rem(me_i + k, insts)}
        return (
            pltpu.make_async_remote_copy(
                src_ref=q_own, dst_ref=q_all.at[me_i], send_sem=q_send.at[k],
                recv_sem=q_recv.at[k], device_id=to, device_id_type=MESH,
            ),
            pltpu.make_async_remote_copy(
                src_ref=t_own, dst_ref=t_all.at[me_i], send_sem=t_send.at[k],
                recv_sem=t_recv.at[k], device_id=to, device_id_type=MESH,
            ),
        )

    for k in range(1, insts):
        for copy in gather_copies(k):
            copy.start()
    q_all[me_i] = q_own[...]
    t_all[me_i] = t_own[...]

    for unit in range(own * groups):
        r, g = unit // groups, unit % groups
        slot, u = unit // units, unit % units
        cut = slice(g * HEAD_SIZE, (g + 1) * HEAD_SIZE)
        products = grouped[g][r * per_group : (r + 1) * per_group] * fresh[0, r : r + 1, cut]
        score = jnp.sum(products, axis=1, keepdims=True)
        place = slice(u * per_group, (u + 1) * per_group)
        fresh_score[slot, place] = jnp.broadcast_to(score, (per_group, HEAD_SIZE))
        fresh_value[slot, place] = jnp.broadcast_to(fresh[1, r : r + 1, cut], (per_group, HEAD_SIZE))

    chunk = 256 // page_tok
    new = lax.broadcasted_iota(jnp.int32, (256, 256), 0)
    old = lax.broadcasted_iota(jnp.int32, (256, 256), 1)
    moves = (new // chunk == lax.rem(old, page_tok)) & (lax.rem(new, chunk) == old // page_tok)
    moves = jnp.where(moves, 1.0, 0.0).astype(jnp.bfloat16)
    for k, copy in enumerate(pool_copies):
        source, target = ((keys, keys_by_token), (values, values_by_token))[k // POOL_PIECES]
        copy.wait()
        base = k % POOL_PIECES * piece
        for c in range(base, base + piece, chunk):
            moved = jnp.dot(
                moves, source[c : c + chunk].reshape(256, source.shape[2]),
                preferred_element_type=jnp.float32,
            )
            target[:, c : c + chunk, :] = moved.astype(jnp.bfloat16).reshape(
                page_tok, chunk, source.shape[2]
            )

    for k in range(1, insts):
        for copy in gather_copies(k):
            copy.wait()

    slot_id = lax.broadcasted_iota(jnp.int32, (slots, 128), 0) + me * slots
    code = jnp.zeros((slots, 128), jnp.int32)
    for i in range(insts):
        packed = t_all[i]
        page_id = packed >> 10
        page_code = packed & 1023
        for r in range(own):
            for b in range(0, columns, 128):
                code += jnp.where(
                    slot_id == page_id[r : r + 1, b : b + 128], page_code[r : r + 1, b : b + 128], 0
                )
    code = jnp.sum(code.astype(jnp.float32).T, axis=0, keepdims=True).astype(jnp.int32)
    slot_owner = jnp.broadcast_to(code >> 5, (BLOCK_ROWS, slots))
    slot_fill = jnp.broadcast_to(code & 31, (BLOCK_ROWS, slots))
    block_row = lax.broadcasted_iota(jnp.int32, (BLOCK_ROWS, slots), 0)
    lane = lax.broadcasted_iota(jnp.int32, (BLOCK_ROWS, 128), 1)

    def tree(join, items):
        while len(items) > 1:
            items = [join(*items[k : k + 2]) for k in range(0, len(items) - 1, 2)] + (
                items[-1:] if len(items) % 2 else []
            )
        return items[0]

    def exchange(to_i, to_p):
        to = to_i * pages + to_p
        return pltpu.make_async_remote_copy(
            src_ref=send.at[to], dst_ref=recv.at[me], send_sem=x_send.at[to],
            recv_sem=x_recv.at[me], device_id={"inst": to_i, "page": to_p}, device_id_type=MESH,
        )

    for pair in range(pairs):
        cut = slice(pair * 2 * HEAD_SIZE, (pair + 1) * 2 * HEAD_SIZE)
        low = q_all[:, 2 * pair].reshape(width, HEAD_SIZE)
        high = q_all[:, 2 * pair + 1].reshape(width, HEAD_SIZE)
        none = jnp.zeros_like(low)
        pair_queries = jnp.concatenate(
            [jnp.concatenate([low, none], axis=1), jnp.concatenate([none, high], axis=1)], axis=0
        )
        scores[pair] = lax.dot_general(
            pair_queries,
            keys_by_token[:, :, cut].reshape(tokens, 2 * HEAD_SIZE),
            (((1,), (1,)), ((), ())),
            preferred_element_type=jnp.float32,
        )

        def weigh(block, pair=pair):
            first = block * BLOCK_ROWS
            if not isinstance(block, int):
                first = pl.multiple_of(first, BLOCK_ROWS)
            row_request = lax.rem(first + block_row, width) // per_group
            filled = jnp.where(slot_owner == row_request, slot_fill, 0)
            masked = [
                jnp.where(
                    filled > t,
                    scores[pair, pl.ds(first, BLOCK_ROWS), t * slots : (t + 1) * slots],
                    LOWEST_SCORE,
                )
                for t in range(page_tok)
            ]
            page_max = tree(jnp.maximum, masked)
            raw = [jnp.exp2((x - page_max) * EXPONENT) for x in masked]
            page_sum = tree(jnp.add, raw)
            local_max = jnp.max(page_max, axis=1, keepdims=True)
            factor = jnp.where(filled > 0, jnp.exp2((page_max - local_max) * EXPONENT), 0.0)
            total = jnp.sum(page_sum * factor, axis=1, keepdims=True)
            for t in range(page_tok):
                scaled = raw[t].astype(jnp.bfloat16).astype(jnp.float32) * factor
                upper = scaled.astype(jnp.bfloat16)
                lower = (scaled - upper.astype(jnp.float32)).astype(jnp.bfloat16)
                at = slice(t * slots, (t + 1) * slots)
                weights[pair, pl.ds(first, BLOCK_ROWS), at] = upper
                weights[pair, pl.ds(lanes + first, BLOCK_ROWS), at] = lower
            columns_of[pair, pl.ds(first, BLOCK_ROWS)] = jnp.where(lane == 0, local_max, total)

        if lanes <= 128:
            for block in range(lanes // BLOCK_ROWS):
                weigh(block)
        else:
            lax.fori_loop(0, lanes // BLOCK_ROWS, lambda block, carry: (weigh(block), carry)[1], 0)
        both = jnp.dot(
            weights[pair], values_by_token[:, :, cut].reshape(tokens, 2 * HEAD_SIZE),
            preferred_element_type=jnp.float32,
        )
        both = both[:lanes] + both[lanes:]
        part = jnp.concatenate([both[:width, :HEAD_SIZE], both[width:, HEAD_SIZE:]], axis=0)
        stats = columns_of[pair].T
        stats = jnp.concatenate(
            [stats[k : k + 1, b * 128 : (b + 1) * 128] for k in range(2) for b in range(stat_rows)],
            axis=0,
        )
        targets = [
            p for p in range(pages) if slot_of(pages, p) * units % groups // 2 == pair
        ]
        for p in targets:
            for i in range(insts):
                send[i * pages + p, unit_rows:] = stats
                for u in range(units):
                    r, g = divmod(slot_of(pages, p) * units + u, groups)
                    start = (g % 2) * width + (i * own + r) * per_group
                    send[i * pages + p, u * per_group : (u + 1) * per_group] = part[
                        start : start + per_group
                    ]

        def start_exchange(k, carry):
            for p in targets:
                exchange(lax.rem(me_i + k, insts), p).start()
            return carry

        if insts <= 4:
            for k in range(1, insts):
                start_exchange(k, 0)
        else:
            lax.fori_loop(1, insts, start_exchange, 0)
        for p in targets:
            @pl.when(me_p != p)
            def _():
                exchange(me_i, p).start()

    recv[me] = send[me]

    def wait_exchange(k, carry):
        other = lax.rem(me + k, devices)
        pltpu.make_async_remote_copy(
            src_ref=send.at[other], dst_ref=recv.at[other], send_sem=x_send.at[other],
            recv_sem=x_recv.at[other],
            device_id={"inst": lax.div(other, pages), "page": lax.rem(other, pages)},
            device_id_type=MESH,
        ).wait()
        return carry

    lax.fori_loop(1, devices, wait_exchange, 0)

    row = lax.broadcasted_iota(jnp.int32, (1, unit_rows, 128), 1)
    lane = lax.broadcasted_iota(jnp.int32, (1, unit_rows, 128), 2)
    unit = me_slot * units + row // per_group
    r, g = unit // groups, lax.rem(unit, groups)
    place = lax.rem(g, 2) * width + (me_i * own + r) * per_group + lax.rem(row, per_group)
    picked = []
    for kind in range(2):
        found = jnp.zeros((devices, unit_rows, 128), jnp.float32)
        for b in range(stat_rows):
            at = unit_rows + kind * stat_rows + b
            found = jnp.where(place == b * 128 + lane, recv[:, at : at + 1, :], found)
        picked.append(jnp.sum(found, axis=2, keepdims=True))
    maxima, totals = picked
    own_score = fresh_score[me_slot]
    top = jnp.maximum(jnp.max(maxima, axis=0), own_score)
    carried = jnp.exp2((maxima - top[None]) * EXPONENT)
    own_weight = jnp.exp2((own_score - top) * EXPONENT)
    denominator = own_weight + jnp.sum(carried * totals, axis=0)
    numerator = own_weight * fresh_value[me_slot] + jnp.sum(
        carried * recv[:, :unit_rows, :], axis=0
    )
    result[...] = (numerator / denominator).astype(result.dtype)

    def result_copy(k):
        return pltpu.make_async_remote_copy(
            src_ref=result, dst_ref=out_hbm.at[me_slot], send_sem=o_send.at[k],
            recv_sem=o_recv.at[k], device_id={"page": lax.rem(me_p + k, pages)},
            device_id_type=MESH,
        )

    for k in range(1, pages):
        result_copy(k).start()
    own_copy = pltpu.make_async_copy(result, out_hbm.at[me_slot], o_own)
    own_copy.start()
    own_copy.wait()
    for k in range(1, pages):
        result_copy(k).wait()


def shards(insts, pages, queries, fresh_key_value, key_value_pool, block_table, lengths):
    own = queries.shape[0]
    slots, page_tok, depth = key_value_pool.shape[1:]
    groups = depth // HEAD_SIZE
    heads = queries.shape[1] // HEAD_SIZE
    per_group = heads // groups
    pairs = groups // 2
    columns = block_table.shape[1]
    lanes = 2 * own * insts * per_group
    devices = insts * pages
    unit_rows = own * heads // pages
    block_rows = unit_rows + 2 * lanes // 128
    hbm = pl.BlockSpec(memory_space=pl.ANY)
    dma = pltpu.SemaphoreType.DMA
    out = pl.pallas_call(
        functools.partial(kernel, insts, pages, groups),
        out_shape=jax.ShapeDtypeStruct((pages, unit_rows, HEAD_SIZE), jnp.bfloat16),
        in_specs=[hbm] * 5,
        out_specs=hbm,
        scratch_shapes=[
            pltpu.VMEM(queries.shape, jnp.bfloat16),
            pltpu.VMEM(fresh_key_value.shape, jnp.bfloat16),
            pltpu.SMEM(lengths.shape, jnp.int32),
            pltpu.VMEM(block_table.shape, jnp.int32),
            pltpu.VMEM((slots, page_tok, depth), jnp.bfloat16),
            pltpu.VMEM((slots, page_tok, depth), jnp.bfloat16),
            pltpu.VMEM((page_tok, slots, depth), jnp.bfloat16),
            pltpu.VMEM((page_tok, slots, depth), jnp.bfloat16),
            pltpu.VMEM((groups, own * per_group, HEAD_SIZE), jnp.bfloat16),
            pltpu.VMEM((insts, groups, own * per_group, HEAD_SIZE), jnp.bfloat16),
            pltpu.VMEM((own, columns), jnp.int32),
            pltpu.VMEM((insts, own, columns), jnp.int32),
            pltpu.VMEM((pairs, lanes, slots * page_tok), jnp.float32),
            pltpu.VMEM((pairs, 2 * lanes, slots * page_tok), jnp.bfloat16),
            pltpu.VMEM((devices, block_rows, 128), jnp.float32),
            pltpu.VMEM((devices, block_rows, 128), jnp.float32),
            pltpu.VMEM((pairs, lanes, 128), jnp.float32),
            pltpu.VMEM((pages, unit_rows, HEAD_SIZE), jnp.float32),
            pltpu.VMEM((pages, unit_rows, HEAD_SIZE), jnp.float32),
            pltpu.VMEM((unit_rows, HEAD_SIZE), jnp.bfloat16),
            dma((4,)), dma((2, POOL_PIECES)),
            dma((insts,)), dma((insts,)), dma((insts,)), dma((insts,)),
            dma((devices,)), dma((devices,)),
            dma((pages,)), dma((pages,)), dma(()),
        ],
        compiler_params=pltpu.CompilerParams(
            collective_id=0, has_side_effects=True, vmem_limit_bytes=56 * 1024 * 1024
        ),
        cost_estimate=pl.CostEstimate(
            flops=8 * slots * page_tok * lanes * HEAD_SIZE * pairs,
            bytes_accessed=4 * slots * page_tok * depth,
            transcendentals=slots * page_tok * lanes * pairs,
        ),
        name="paged_attention",
    )(queries, fresh_key_value, lengths, block_table, key_value_pool)
    return out.reshape(own, heads * HEAD_SIZE)


def solution(mesh):
    return jax.shard_map(
        functools.partial(shards, mesh.shape["inst"], mesh.shape["page"]),
        mesh=mesh,
        in_specs=(
            P("inst", "head"),
            P(None, "inst", "head"),
            P(None, ("inst", "page"), None, "head"),
            P("inst", None),
            P("inst"),
        ),
        out_specs=P("inst", "head"),
        check_vma=False,
    )
```

```python
import functools
import math

import jax
import jax.numpy as jnp
from jax import lax
from jax.experimental import pallas as pl
from jax.experimental.pallas import tpu as pltpu
from jax.sharding import PartitionSpec as P

HEAD_SIZE = 128
LOWEST_SCORE = -1e30
EXPONENT = math.log2(math.e) / math.sqrt(HEAD_SIZE)
BLOCK_ROWS = 16
POOL_PIECES = 4
MESH = pl.DeviceIdType.MESH


def kernel(
    insts, pages, groups,
    q_hbm, fresh_hbm, len_hbm, table_hbm, pool_hbm, out_hbm,
    q_ref, fresh_ref, len_ref, table_ref,
    keys, values, keys_by_token, values_by_token, q_own, q_all, t_own, t_all,
    scores, weights, send, recv,
    columns_of, fresh_score, fresh_value, result,
    in_sem, pool_sem, q_send, q_recv, t_send, t_recv, x_send, x_recv, o_send, o_recv, o_own,
):
    own = q_ref.shape[0]
    heads = q_ref.shape[1] // HEAD_SIZE
    per_group = heads // groups
    pairs = groups // 2
    requests = own * insts
    columns = table_ref.shape[1]
    slots, page_tok = keys.shape[0], keys.shape[1]
    tokens = slots * page_tok
    width = requests * per_group
    lanes = 2 * width
    stat_rows = lanes // 128
    devices = insts * pages
    rows = own * per_group
    middle = pages // 2 - 1

    me_i = lax.axis_index("inst")
    me_p = lax.axis_index("page")
    me = me_i * pages + me_p
    finishes = (me_p == middle) | (me_p == middle + 1)
    side = lax.rem(me_p + pages - middle, 2)

    barrier = pltpu.get_barrier_semaphore()

    def greet(p, first):
        def one(k, carry):
            pl.semaphore_signal(
                barrier, inc=1, device_id={"inst": lax.rem(me_i + k, insts), "page": p},
                device_id_type=MESH,
            )
            return carry

        lax.fori_loop(first, insts, one, 0)

    greet(me_p, 1)

    @pl.when(finishes)
    def _():
        for k in range(1, pages):
            greet(lax.rem(me_p + k, pages), 0)

    @pl.when(jnp.logical_not(finishes))
    def _():
        for j in range(2):
            greet(middle + j, 0)

    small = [
        pltpu.make_async_copy(source, target, in_sem.at[k])
        for k, (source, target) in enumerate(
            [(q_hbm, q_ref), (len_hbm, len_ref), (table_hbm, table_ref), (fresh_hbm, fresh_ref)]
        )
    ]
    for copy in small:
        copy.start()
    piece = slots // POOL_PIECES
    pool_copies = [
        pltpu.make_async_copy(
            pool_hbm.at[kind, pl.ds(c * piece, piece)], target.at[pl.ds(c * piece, piece)],
            pool_sem.at[kind, c],
        )
        for kind, target in enumerate((keys, values))
        for c in range(POOL_PIECES)
    ]
    for copy in pool_copies:
        copy.start()
    for copy in small:
        copy.wait()

    q = q_ref[...].astype(jnp.float32)
    fresh = fresh_ref[...].astype(jnp.float32)
    grouped = []
    for g in range(groups):
        stacked = jnp.concatenate(
            [
                q[r : r + 1, (g * per_group + h) * HEAD_SIZE : (g * per_group + h + 1) * HEAD_SIZE]
                for r in range(own)
                for h in range(per_group)
            ],
            axis=0,
        )
        grouped.append(stacked)
        q_own[g] = stacked.astype(jnp.bfloat16)
    column = lax.broadcasted_iota(jnp.int32, (own, columns), 1)
    row = lax.broadcasted_iota(jnp.int32, (own, columns), 0)
    length = jnp.zeros((own, columns), jnp.int32)
    for r in range(own):
        length = jnp.where(row == r, len_ref[r], length)
    fill = jnp.clip(length - column * page_tok, 0, page_tok)
    t_own[...] = jnp.where(
        fill > 0, table_ref[...] * 1024 + (me_i * own + row) * 32 + fill, -1
    )

    @pl.when(finishes)
    def _():
        pl.semaphore_wait(barrier, devices - 1)

    @pl.when(jnp.logical_not(finishes))
    def _():
        pl.semaphore_wait(barrier, 3 * insts - 1)

    def gather_copies(k):
        to = {"inst": lax.rem(me_i + k, insts)}
        return (
            pltpu.make_async_remote_copy(
                src_ref=q_own, dst_ref=q_all.at[me_i], send_sem=q_send.at[k],
                recv_sem=q_recv.at[k], device_id=to, device_id_type=MESH,
            ),
            pltpu.make_async_remote_copy(
                src_ref=t_own, dst_ref=t_all.at[me_i], send_sem=t_send.at[k],
                recv_sem=t_recv.at[k], device_id=to, device_id_type=MESH,
            ),
        )

    for k in range(1, insts):
        for copy in gather_copies(k):
            copy.start()
    q_all[me_i] = q_own[...]
    t_all[me_i] = t_own[...]

    for g in range(groups):
        cut = slice(g * HEAD_SIZE, (g + 1) * HEAD_SIZE)
        for r in range(own):
            place = slice(r * per_group, (r + 1) * per_group)
            products = grouped[g][place] * fresh[0, r : r + 1, cut]
            score = jnp.sum(products, axis=1, keepdims=True)
            fresh_score[g, place] = jnp.broadcast_to(score, (per_group, HEAD_SIZE))
            fresh_value[g, place] = jnp.broadcast_to(fresh[1, r : r + 1, cut], (per_group, HEAD_SIZE))

    chunk = 256 // page_tok
    new = lax.broadcasted_iota(jnp.int32, (256, 256), 0)
    old = lax.broadcasted_iota(jnp.int32, (256, 256), 1)
    moves = (new // chunk == lax.rem(old, page_tok)) & (lax.rem(new, chunk) == old // page_tok)
    moves = jnp.where(moves, 1.0, 0.0).astype(jnp.bfloat16)
    for k, copy in enumerate(pool_copies):
        source, target = ((keys, keys_by_token), (values, values_by_token))[k // POOL_PIECES]
        copy.wait()
        base = k % POOL_PIECES * piece
        for c in range(base, base + piece, chunk):
            moved = jnp.dot(
                moves, source[c : c + chunk].reshape(256, source.shape[2]),
                preferred_element_type=jnp.float32,
            )
            target[:, c : c + chunk, :] = moved.astype(jnp.bfloat16).reshape(
                page_tok, chunk, source.shape[2]
            )

    for k in range(1, insts):
        for copy in gather_copies(k):
            copy.wait()

    slot_id = lax.broadcasted_iota(jnp.int32, (slots, 128), 0) + me * slots
    code = jnp.zeros((slots, 128), jnp.int32)
    for i in range(insts):
        packed = t_all[i]
        page_id = packed >> 10
        page_code = packed & 1023
        for r in range(own):
            for b in range(0, columns, 128):
                code += jnp.where(
                    slot_id == page_id[r : r + 1, b : b + 128], page_code[r : r + 1, b : b + 128], 0
                )
    code = jnp.sum(code.astype(jnp.float32).T, axis=0, keepdims=True).astype(jnp.int32)
    slot_owner = jnp.broadcast_to(code >> 5, (BLOCK_ROWS, slots))
    slot_fill = jnp.broadcast_to(code & 31, (BLOCK_ROWS, slots))
    block_row = lax.broadcasted_iota(jnp.int32, (BLOCK_ROWS, slots), 0)
    lane = lax.broadcasted_iota(jnp.int32, (BLOCK_ROWS, 128), 1)

    def tree(join, items):
        while len(items) > 1:
            items = [join(*items[k : k + 2]) for k in range(0, len(items) - 1, 2)] + (
                items[-1:] if len(items) % 2 else []
            )
        return items[0]

    def exchange(pair, j, to_i):
        return pltpu.make_async_remote_copy(
            src_ref=send.at[pair, j, to_i], dst_ref=recv.at[pair, me],
            send_sem=x_send.at[pair, j, to_i], recv_sem=x_recv.at[pair, me],
            device_id={"inst": to_i, "page": middle + j}, device_id_type=MESH,
        )

    def all_exchanges(pair, act):
        def one(k, carry):
            for j in range(2):
                act(exchange(pair, j, lax.rem(me_i + k, insts)))
            return carry

        if insts <= 4:
            for k in range(1, insts):
                one(k, 0)
        else:
            lax.fori_loop(1, insts, one, 0)
        for j in range(2):
            @pl.when(me_p != middle + j)
            def _():
                act(exchange(pair, j, me_i))

    for pair in range(pairs):
        cut = slice(pair * 2 * HEAD_SIZE, (pair + 1) * 2 * HEAD_SIZE)
        low = q_all[:, 2 * pair].reshape(width, HEAD_SIZE)
        high = q_all[:, 2 * pair + 1].reshape(width, HEAD_SIZE)
        none = jnp.zeros_like(low)
        pair_queries = jnp.concatenate(
            [jnp.concatenate([low, none], axis=1), jnp.concatenate([none, high], axis=1)], axis=0
        )
        scores[pair] = lax.dot_general(
            pair_queries,
            keys_by_token[:, :, cut].reshape(tokens, 2 * HEAD_SIZE),
            (((1,), (1,)), ((), ())),
            preferred_element_type=jnp.float32,
        )

    for pair in range(pairs):
        cut = slice(pair * 2 * HEAD_SIZE, (pair + 1) * 2 * HEAD_SIZE)

        def weigh(block, pair=pair):
            first = block * BLOCK_ROWS
            if not isinstance(block, int):
                first = pl.multiple_of(first, BLOCK_ROWS)
            row_request = lax.rem(first + block_row, width) // per_group
            filled = jnp.where(slot_owner == row_request, slot_fill, 0)
            masked = [
                jnp.where(
                    filled > t,
                    scores[pair, pl.ds(first, BLOCK_ROWS), t * slots : (t + 1) * slots],
                    LOWEST_SCORE,
                )
                for t in range(page_tok)
            ]
            page_max = tree(jnp.maximum, masked)
            raw = [jnp.exp2((x - page_max) * EXPONENT) for x in masked]
            page_sum = tree(jnp.add, raw)
            local_max = jnp.max(page_max, axis=1, keepdims=True)
            factor = jnp.where(filled > 0, jnp.exp2((page_max - local_max) * EXPONENT), 0.0)
            total = jnp.sum(page_sum * factor, axis=1, keepdims=True)
            for t in range(page_tok):
                scaled = raw[t].astype(jnp.bfloat16).astype(jnp.float32) * factor
                upper = scaled.astype(jnp.bfloat16)
                lower = (scaled - upper.astype(jnp.float32)).astype(jnp.bfloat16)
                at = slice(t * slots, (t + 1) * slots)
                weights[pair, pl.ds(first, BLOCK_ROWS), at] = upper
                weights[pair, pl.ds(lanes + first, BLOCK_ROWS), at] = lower
            columns_of[pair, pl.ds(first, BLOCK_ROWS)] = jnp.where(lane == 0, local_max, total)

        if lanes <= 128:
            for block in range(lanes // BLOCK_ROWS):
                weigh(block)
        else:
            lax.fori_loop(0, lanes // BLOCK_ROWS, lambda block, carry: (weigh(block), carry)[1], 0)
        both = jnp.dot(
            weights[pair], values_by_token[:, :, cut].reshape(tokens, 2 * HEAD_SIZE),
            preferred_element_type=jnp.float32,
        )
        both = both[:lanes] + both[lanes:]
        part = jnp.concatenate([both[:width, :HEAD_SIZE], both[width:, HEAD_SIZE:]], axis=0)
        stats = columns_of[pair].T
        stats = jnp.concatenate(
            [stats[k : k + 1, b * 128 : (b + 1) * 128] for k in range(2) for b in range(stat_rows)],
            axis=0,
        )
        for i in range(insts):
            for j in range(2):
                start = j * width + i * rows
                send[pair, j, i, :rows] = part[start : start + rows]
                send[pair, j, i, rows:] = stats
        all_exchanges(pair, lambda copy: copy.start())

    def result_copy(pair, k):
        at = pl.ds(pl.multiple_of((2 * pair + side) * per_group * HEAD_SIZE, 128), per_group * HEAD_SIZE)
        return pltpu.make_async_remote_copy(
            src_ref=result.at[pair], dst_ref=out_hbm.at[:, at], send_sem=o_send.at[pair, k],
            recv_sem=o_recv.at[pair, side], device_id={"page": lax.rem(me_p + k, pages)},
            device_id_type=MESH,
        )

    def own_copy(pair):
        at = pl.ds(pl.multiple_of((2 * pair + side) * per_group * HEAD_SIZE, 128), per_group * HEAD_SIZE)
        return pltpu.make_async_copy(result.at[pair], out_hbm.at[:, at], o_own.at[pair])

    @pl.when(finishes)
    def _():
        row = lax.broadcasted_iota(jnp.int32, (1, rows, 128), 1)
        lane = lax.broadcasted_iota(jnp.int32, (1, rows, 128), 2)
        place = side * width + me_i * rows + row
        for pair in range(pairs):
            recv[pair, me] = send[pair, side, me_i]

            def wait_exchange(k, carry, pair=pair):
                other = lax.rem(me + k, devices)
                pltpu.make_async_remote_copy(
                    src_ref=send.at[pair, 0, 0], dst_ref=recv.at[pair, other],
                    send_sem=x_send.at[pair, 0, 0], recv_sem=x_recv.at[pair, other],
                    device_id={"inst": lax.div(other, pages), "page": lax.rem(other, pages)},
                    device_id_type=MESH,
                ).wait_recv()
                return carry

            lax.fori_loop(1, devices, wait_exchange, 0)
            picked = []
            for kind in range(2):
                found = jnp.zeros((devices, rows, 128), jnp.float32)
                for b in range(stat_rows):
                    at = rows + kind * stat_rows + b
                    found = jnp.where(place == b * 128 + lane, recv[pair, :, at : at + 1, :], found)
                picked.append(jnp.sum(found, axis=2, keepdims=True))
            maxima, totals = picked
            own_score = fresh_score[2 * pair + side]
            top = jnp.maximum(jnp.max(maxima, axis=0), own_score)
            carried = jnp.exp2((maxima - top[None]) * EXPONENT)
            own_weight = jnp.exp2((own_score - top) * EXPONENT)
            denominator = own_weight + jnp.sum(carried * totals, axis=0)
            numerator = own_weight * fresh_value[2 * pair + side] + jnp.sum(
                carried * recv[pair, :, :rows, :], axis=0
            )
            attn = numerator / denominator
            attn = jnp.concatenate(
                [
                    jnp.concatenate(
                        [attn[r * per_group + h : r * per_group + h + 1] for h in range(per_group)],
                        axis=1,
                    )
                    for r in range(own)
                ],
                axis=0,
            )
            result[pair] = attn.astype(result.dtype)
            for k in range(1, pages):
                result_copy(pair, k).start()
            own_copy(pair).start()

    for pair in range(pairs):
        for j in range(2):
            @pl.when(me_p != middle + j)
            def _():
                at = slice(
                    (2 * pair + j) * per_group * HEAD_SIZE, (2 * pair + j + 1) * per_group * HEAD_SIZE
                )
                pltpu.make_async_remote_copy(
                    src_ref=result.at[pair], dst_ref=out_hbm.at[:, at], send_sem=o_send.at[pair, 0],
                    recv_sem=o_recv.at[pair, j], device_id={"page": middle + j},
                    device_id_type=MESH,
                ).wait_recv()

    @pl.when(finishes)
    def _():
        for pair in range(pairs):
            own_copy(pair).wait()
            for k in range(1, pages):
                result_copy(pair, k).wait_send()

    for pair in range(pairs):
        all_exchanges(pair, lambda copy: copy.wait_send())


def shards(insts, pages, queries, fresh_key_value, key_value_pool, block_table, lengths):
    own = queries.shape[0]
    slots, page_tok, depth = key_value_pool.shape[1:]
    groups = depth // HEAD_SIZE
    heads = queries.shape[1] // HEAD_SIZE
    per_group = heads // groups
    pairs = groups // 2
    columns = block_table.shape[1]
    lanes = 2 * own * insts * per_group
    devices = insts * pages
    rows = own * per_group
    block_rows = rows + 2 * lanes // 128
    hbm = pl.BlockSpec(memory_space=pl.ANY)
    dma = pltpu.SemaphoreType.DMA
    return pl.pallas_call(
        functools.partial(kernel, insts, pages, groups),
        out_shape=jax.ShapeDtypeStruct(queries.shape, jnp.bfloat16),
        in_specs=[hbm] * 5,
        out_specs=hbm,
        scratch_shapes=[
            pltpu.VMEM(queries.shape, jnp.bfloat16),
            pltpu.VMEM(fresh_key_value.shape, jnp.bfloat16),
            pltpu.SMEM(lengths.shape, jnp.int32),
            pltpu.VMEM(block_table.shape, jnp.int32),
            pltpu.VMEM((slots, page_tok, depth), jnp.bfloat16),
            pltpu.VMEM((slots, page_tok, depth), jnp.bfloat16),
            pltpu.VMEM((page_tok, slots, depth), jnp.bfloat16),
            pltpu.VMEM((page_tok, slots, depth), jnp.bfloat16),
            pltpu.VMEM((groups, own * per_group, HEAD_SIZE), jnp.bfloat16),
            pltpu.VMEM((insts, groups, own * per_group, HEAD_SIZE), jnp.bfloat16),
            pltpu.VMEM((own, columns), jnp.int32),
            pltpu.VMEM((insts, own, columns), jnp.int32),
            pltpu.VMEM((pairs, lanes, slots * page_tok), jnp.float32),
            pltpu.VMEM((pairs, 2 * lanes, slots * page_tok), jnp.bfloat16),
            pltpu.VMEM((pairs, 2, insts, block_rows, 128), jnp.float32),
            pltpu.VMEM((pairs, devices, block_rows, 128), jnp.float32),
            pltpu.VMEM((pairs, lanes, 128), jnp.float32),
            pltpu.VMEM((groups, rows, HEAD_SIZE), jnp.float32),
            pltpu.VMEM((groups, rows, HEAD_SIZE), jnp.float32),
            pltpu.VMEM((pairs, own, per_group * HEAD_SIZE), jnp.bfloat16),
            dma((4,)), dma((2, POOL_PIECES)),
            dma((insts,)), dma((insts,)), dma((insts,)), dma((insts,)),
            dma((pairs, 2, insts)), dma((pairs, devices)),
            dma((pairs, pages)), dma((pairs, 2)), dma((pairs,)),
        ],
        compiler_params=pltpu.CompilerParams(
            collective_id=0, has_side_effects=True, vmem_limit_bytes=56 * 1024 * 1024
        ),
        cost_estimate=pl.CostEstimate(
            flops=8 * slots * page_tok * lanes * HEAD_SIZE * pairs,
            bytes_accessed=4 * slots * page_tok * depth,
            transcendentals=slots * page_tok * lanes * pairs,
        ),
        name="paged_attention",
    )(queries, fresh_key_value, lengths, block_table, key_value_pool)


def solution(mesh):
    return jax.shard_map(
        functools.partial(shards, mesh.shape["inst"], mesh.shape["page"]),
        mesh=mesh,
        in_specs=(
            P("inst", "head"),
            P(None, "inst", "head"),
            P(None, ("inst", "page"), None, "head"),
            P("inst", None),
            P("inst"),
        ),
        out_specs=P("inst", "head"),
        check_vma=False,
    )
```

```python
import functools
import math

import jax
import jax.numpy as jnp
from jax import lax
from jax.experimental import pallas as pl
from jax.experimental.pallas import tpu as pltpu
from jax.sharding import PartitionSpec as P

HEAD_SIZE = 128
LOWEST_SCORE = -1e30
EXPONENT = math.log2(math.e) / math.sqrt(HEAD_SIZE)
BLOCK_ROWS = 16
POOL_PIECES = 4
MESH = pl.DeviceIdType.MESH


def kernel(
    insts, pages, groups,
    q_hbm, fresh_hbm, len_hbm, table_hbm, pool_hbm, out_hbm,
    q_ref, fresh_ref, len_ref, table_ref,
    keys, values, keys_by_token, values_by_token, q_own, q_all, t_own, t_all,
    scores, weights, send, recv,
    columns_of, fresh_score, fresh_value, result,
    in_sem, pool_sem, q_send, q_recv, t_send, t_recv, x_send, x_recv, o_send, o_recv, o_own,
):
    own = q_ref.shape[0]
    heads = q_ref.shape[1] // HEAD_SIZE
    per_group = heads // groups
    pairs = groups // 2
    requests = own * insts
    columns = table_ref.shape[1]
    slots, page_tok = keys.shape[0], keys.shape[1]
    tokens = slots * page_tok
    width = requests * per_group
    lanes = 2 * width
    stat_rows = lanes // 128
    devices = insts * pages
    rows = own * per_group
    middle = pages // 2 - 1

    me_i = lax.axis_index("inst")
    me_p = lax.axis_index("page")
    me = me_i * pages + me_p
    finishes = (me_p == middle) | (me_p == middle + 1)
    side = lax.rem(me_p + pages - middle, 2)

    barrier = pltpu.get_barrier_semaphore()

    def greet(p, first):
        def one(k, carry):
            pl.semaphore_signal(
                barrier, inc=1, device_id={"inst": lax.rem(me_i + k, insts), "page": p},
                device_id_type=MESH,
            )
            return carry

        lax.fori_loop(first, insts, one, 0)

    greet(me_p, 1)

    @pl.when(finishes)
    def _():
        for k in range(1, pages):
            greet(lax.rem(me_p + k, pages), 0)

    @pl.when(jnp.logical_not(finishes))
    def _():
        for j in range(2):
            greet(middle + j, 0)

    small = [
        pltpu.make_async_copy(source, target, in_sem.at[k])
        for k, (source, target) in enumerate(
            [(q_hbm, q_ref), (len_hbm, len_ref), (table_hbm, table_ref), (fresh_hbm, fresh_ref)]
        )
    ]
    for copy in small:
        copy.start()
    piece = slots // POOL_PIECES
    pool_copies = [
        pltpu.make_async_copy(
            pool_hbm.at[kind, pl.ds(c * piece, piece)], target.at[pl.ds(c * piece, piece)],
            pool_sem.at[kind, c],
        )
        for kind, target in enumerate((keys, values))
        for c in range(POOL_PIECES)
    ]
    for copy in pool_copies:
        copy.start()
    for copy in small:
        copy.wait()

    q = q_ref[...].astype(jnp.float32)
    fresh = fresh_ref[...].astype(jnp.float32)
    grouped = []
    for g in range(groups):
        stacked = jnp.concatenate(
            [
                q[r : r + 1, (g * per_group + h) * HEAD_SIZE : (g * per_group + h + 1) * HEAD_SIZE]
                for r in range(own)
                for h in range(per_group)
            ],
            axis=0,
        )
        grouped.append(stacked)
        q_own[g] = stacked.astype(jnp.bfloat16)
    column = lax.broadcasted_iota(jnp.int32, (own, columns), 1)
    row = lax.broadcasted_iota(jnp.int32, (own, columns), 0)
    length = jnp.zeros((own, columns), jnp.int32)
    for r in range(own):
        length = jnp.where(row == r, len_ref[r], length)
    fill = jnp.clip(length - column * page_tok, 0, page_tok)
    t_own[...] = jnp.where(
        fill > 0, table_ref[...] * 1024 + (me_i * own + row) * 32 + fill, -1
    )

    @pl.when(finishes)
    def _():
        pl.semaphore_wait(barrier, devices - 1)

    @pl.when(jnp.logical_not(finishes))
    def _():
        pl.semaphore_wait(barrier, 3 * insts - 1)

    def gather_copies(k):
        to = {"inst": lax.rem(me_i + k, insts)}
        return (
            pltpu.make_async_remote_copy(
                src_ref=q_own, dst_ref=q_all.at[me_i], send_sem=q_send.at[k],
                recv_sem=q_recv.at[k], device_id=to, device_id_type=MESH,
            ),
            pltpu.make_async_remote_copy(
                src_ref=t_own, dst_ref=t_all.at[me_i], send_sem=t_send.at[k],
                recv_sem=t_recv.at[k], device_id=to, device_id_type=MESH,
            ),
        )

    for k in range(1, insts):
        for copy in gather_copies(k):
            copy.start()
    q_all[me_i] = q_own[...]
    t_all[me_i] = t_own[...]

    for g in range(groups):
        cut = slice(g * HEAD_SIZE, (g + 1) * HEAD_SIZE)
        for r in range(own):
            place = slice(r * per_group, (r + 1) * per_group)
            products = grouped[g][place] * fresh[0, r : r + 1, cut]
            score = jnp.sum(products, axis=1, keepdims=True)
            fresh_score[g, place] = jnp.broadcast_to(score, (per_group, HEAD_SIZE))
            fresh_value[g, place] = jnp.broadcast_to(fresh[1, r : r + 1, cut], (per_group, HEAD_SIZE))

    chunk = 256 // page_tok
    new = lax.broadcasted_iota(jnp.int32, (256, 256), 0)
    old = lax.broadcasted_iota(jnp.int32, (256, 256), 1)
    moves = (new // chunk == lax.rem(old, page_tok)) & (lax.rem(new, chunk) == old // page_tok)
    moves = jnp.where(moves, 1.0, 0.0).astype(jnp.bfloat16)
    for k, copy in enumerate(pool_copies):
        source, target = ((keys, keys_by_token), (values, values_by_token))[k // POOL_PIECES]
        copy.wait()
        base = k % POOL_PIECES * piece
        for c in range(base, base + piece, chunk):
            moved = jnp.dot(
                moves, source[c : c + chunk].reshape(256, source.shape[2]),
                preferred_element_type=jnp.float32,
            )
            target[:, c : c + chunk, :] = moved.astype(jnp.bfloat16).reshape(
                page_tok, chunk, source.shape[2]
            )

    for k in range(1, insts):
        for copy in gather_copies(k):
            copy.wait()

    slot_id = lax.broadcasted_iota(jnp.int32, (slots, 128), 0) + me * slots
    code = jnp.zeros((slots, 128), jnp.int32)
    for i in range(insts):
        packed = t_all[i]
        page_id = packed >> 10
        page_code = packed & 1023
        for r in range(own):
            for b in range(0, columns, 128):
                code += jnp.where(
                    slot_id == page_id[r : r + 1, b : b + 128], page_code[r : r + 1, b : b + 128], 0
                )
    code = jnp.sum(code.astype(jnp.float32).T, axis=0, keepdims=True).astype(jnp.int32)
    slot_owner = jnp.broadcast_to(code >> 5, (BLOCK_ROWS, slots))
    slot_fill = jnp.broadcast_to(code & 31, (BLOCK_ROWS, slots))
    block_row = lax.broadcasted_iota(jnp.int32, (BLOCK_ROWS, slots), 0)
    lane = lax.broadcasted_iota(jnp.int32, (BLOCK_ROWS, 128), 1)

    def tree(join, items):
        while len(items) > 1:
            items = [join(*items[k : k + 2]) for k in range(0, len(items) - 1, 2)] + (
                items[-1:] if len(items) % 2 else []
            )
        return items[0]

    def exchange(pair, j, to_i):
        return pltpu.make_async_remote_copy(
            src_ref=send.at[pair, j, to_i], dst_ref=recv.at[pair, me],
            send_sem=x_send.at[pair, j, to_i], recv_sem=x_recv.at[pair, me],
            device_id={"inst": to_i, "page": middle + j}, device_id_type=MESH,
        )

    def all_exchanges(pair, act):
        def one(k, carry):
            for j in range(2):
                act(exchange(pair, j, lax.rem(me_i + k, insts)))
            return carry

        if insts <= 4:
            for k in range(1, insts):
                one(k, 0)
        else:
            lax.fori_loop(1, insts, one, 0)
        for j in range(2):
            @pl.when(me_p != middle + j)
            def _():
                act(exchange(pair, j, me_i))

    for pair in range(pairs):
        cut = slice(pair * 2 * HEAD_SIZE, (pair + 1) * 2 * HEAD_SIZE)
        low = q_all[:, 2 * pair].reshape(width, HEAD_SIZE)
        high = q_all[:, 2 * pair + 1].reshape(width, HEAD_SIZE)
        none = jnp.zeros_like(low)
        pair_queries = jnp.concatenate(
            [jnp.concatenate([low, none], axis=1), jnp.concatenate([none, high], axis=1)], axis=0
        )
        scores[pair] = lax.dot_general(
            pair_queries,
            keys_by_token[:, :, cut].reshape(tokens, 2 * HEAD_SIZE),
            (((1,), (1,)), ((), ())),
            preferred_element_type=jnp.float32,
        )

    for pair in range(pairs):
        cut = slice(pair * 2 * HEAD_SIZE, (pair + 1) * 2 * HEAD_SIZE)

        def weigh(block, pair=pair):
            first = block * BLOCK_ROWS
            if not isinstance(block, int):
                first = pl.multiple_of(first, BLOCK_ROWS)
            row_request = lax.rem(first + block_row, width) // per_group
            owned = (slot_owner == row_request) & (slot_fill > 0)
            masked = [
                jnp.where(
                    slot_fill > t,
                    scores[pair, pl.ds(first, BLOCK_ROWS), t * slots : (t + 1) * slots],
                    LOWEST_SCORE,
                )
                for t in range(page_tok)
            ]
            page_max = tree(jnp.maximum, masked)
            raw = [jnp.exp2((x - page_max) * EXPONENT) for x in masked]
            page_sum = tree(jnp.add, raw)
            local_max = jnp.max(
                jnp.where(owned, page_max, LOWEST_SCORE), axis=1, keepdims=True
            )
            factor = jnp.where(owned, jnp.exp2((page_max - local_max) * EXPONENT), 0.0)
            total = jnp.sum(page_sum * factor, axis=1, keepdims=True)
            for t in range(page_tok):
                scaled = raw[t].astype(jnp.bfloat16).astype(jnp.float32) * factor
                upper = scaled.astype(jnp.bfloat16)
                lower = (scaled - upper.astype(jnp.float32)).astype(jnp.bfloat16)
                at = slice(t * slots, (t + 1) * slots)
                weights[pair, pl.ds(first, BLOCK_ROWS), at] = upper
                weights[pair, pl.ds(lanes + first, BLOCK_ROWS), at] = lower
            columns_of[pair, pl.ds(first, BLOCK_ROWS)] = jnp.where(lane == 0, local_max, total)

        if lanes <= 128:
            for block in range(lanes // BLOCK_ROWS):
                weigh(block)
        else:
            lax.fori_loop(0, lanes // BLOCK_ROWS, lambda block, carry: (weigh(block), carry)[1], 0)
        both = jnp.dot(
            weights[pair], values_by_token[:, :, cut].reshape(tokens, 2 * HEAD_SIZE),
            preferred_element_type=jnp.float32,
        )
        both = both[:lanes] + both[lanes:]
        part = jnp.concatenate([both[:width, :HEAD_SIZE], both[width:, HEAD_SIZE:]], axis=0)
        stats = columns_of[pair].T
        stats = jnp.concatenate(
            [stats[k : k + 1, b * 128 : (b + 1) * 128] for k in range(2) for b in range(stat_rows)],
            axis=0,
        )
        for i in range(insts):
            for j in range(2):
                start = j * width + i * rows
                send[pair, j, i, :rows] = part[start : start + rows]
                send[pair, j, i, rows:] = stats
        all_exchanges(pair, lambda copy: copy.start())

    def result_copy(pair, k):
        at = pl.ds(pl.multiple_of((2 * pair + side) * per_group * HEAD_SIZE, 128), per_group * HEAD_SIZE)
        return pltpu.make_async_remote_copy(
            src_ref=result.at[pair], dst_ref=out_hbm.at[:, at], send_sem=o_send.at[pair, k],
            recv_sem=o_recv.at[pair, side], device_id={"page": lax.rem(me_p + k, pages)},
            device_id_type=MESH,
        )

    def own_copy(pair):
        at = pl.ds(pl.multiple_of((2 * pair + side) * per_group * HEAD_SIZE, 128), per_group * HEAD_SIZE)
        return pltpu.make_async_copy(result.at[pair], out_hbm.at[:, at], o_own.at[pair])

    @pl.when(finishes)
    def _():
        row = lax.broadcasted_iota(jnp.int32, (1, rows, 128), 1)
        lane = lax.broadcasted_iota(jnp.int32, (1, rows, 128), 2)
        place = side * width + me_i * rows + row
        for pair in range(pairs):
            recv[pair, me] = send[pair, side, me_i]

            def wait_exchange(k, carry, pair=pair):
                other = lax.rem(me + k, devices)
                pltpu.make_async_remote_copy(
                    src_ref=send.at[pair, 0, 0], dst_ref=recv.at[pair, other],
                    send_sem=x_send.at[pair, 0, 0], recv_sem=x_recv.at[pair, other],
                    device_id={"inst": lax.div(other, pages), "page": lax.rem(other, pages)},
                    device_id_type=MESH,
                ).wait_recv()
                return carry

            lax.fori_loop(1, devices, wait_exchange, 0)
            picked = []
            for kind in range(2):
                found = jnp.zeros((devices, rows, 128), jnp.float32)
                for b in range(stat_rows):
                    at = rows + kind * stat_rows + b
                    found = jnp.where(place == b * 128 + lane, recv[pair, :, at : at + 1, :], found)
                picked.append(jnp.sum(found, axis=2, keepdims=True))
            maxima, totals = picked
            own_score = fresh_score[2 * pair + side]
            top = jnp.maximum(jnp.max(maxima, axis=0), own_score)
            carried = jnp.exp2((maxima - top[None]) * EXPONENT)
            own_weight = jnp.exp2((own_score - top) * EXPONENT)
            denominator = own_weight + jnp.sum(carried * totals, axis=0)
            numerator = own_weight * fresh_value[2 * pair + side] + jnp.sum(
                carried * recv[pair, :, :rows, :], axis=0
            )
            attn = numerator / denominator
            attn = jnp.concatenate(
                [
                    jnp.concatenate(
                        [attn[r * per_group + h : r * per_group + h + 1] for h in range(per_group)],
                        axis=1,
                    )
                    for r in range(own)
                ],
                axis=0,
            )
            result[pair] = attn.astype(result.dtype)
            for k in range(1, pages):
                result_copy(pair, k).start()
            own_copy(pair).start()

    for pair in range(pairs):
        for j in range(2):
            @pl.when(me_p != middle + j)
            def _():
                at = slice(
                    (2 * pair + j) * per_group * HEAD_SIZE, (2 * pair + j + 1) * per_group * HEAD_SIZE
                )
                pltpu.make_async_remote_copy(
                    src_ref=result.at[pair], dst_ref=out_hbm.at[:, at], send_sem=o_send.at[pair, 0],
                    recv_sem=o_recv.at[pair, j], device_id={"page": middle + j},
                    device_id_type=MESH,
                ).wait_recv()

    @pl.when(finishes)
    def _():
        for pair in range(pairs):
            own_copy(pair).wait()
            for k in range(1, pages):
                result_copy(pair, k).wait_send()

    for pair in range(pairs):
        all_exchanges(pair, lambda copy: copy.wait_send())


def settle(source, target, sem):
    copy = pltpu.make_async_copy(source, target, sem)
    copy.start()
    copy.wait()


def shards(insts, pages, queries, fresh_key_value, key_value_pool, block_table, lengths):
    own = queries.shape[0]
    slots, page_tok, depth = key_value_pool.shape[1:]
    groups = depth // HEAD_SIZE
    heads = queries.shape[1] // HEAD_SIZE
    per_group = heads // groups
    pairs = groups // 2
    columns = block_table.shape[1]
    lanes = 2 * own * insts * per_group
    devices = insts * pages
    rows = own * per_group
    block_rows = rows + 2 * lanes // 128
    hbm = pl.BlockSpec(memory_space=pl.ANY)
    dma = pltpu.SemaphoreType.DMA
    out = pl.pallas_call(
        functools.partial(kernel, insts, pages, groups),
        out_shape=jax.ShapeDtypeStruct(queries.shape, jnp.bfloat16),
        in_specs=[hbm] * 5,
        out_specs=hbm,
        scratch_shapes=[
            pltpu.VMEM(queries.shape, jnp.bfloat16),
            pltpu.VMEM(fresh_key_value.shape, jnp.bfloat16),
            pltpu.SMEM(lengths.shape, jnp.int32),
            pltpu.VMEM(block_table.shape, jnp.int32),
            pltpu.VMEM((slots, page_tok, depth), jnp.bfloat16),
            pltpu.VMEM((slots, page_tok, depth), jnp.bfloat16),
            pltpu.VMEM((page_tok, slots, depth), jnp.bfloat16),
            pltpu.VMEM((page_tok, slots, depth), jnp.bfloat16),
            pltpu.VMEM((groups, own * per_group, HEAD_SIZE), jnp.bfloat16),
            pltpu.VMEM((insts, groups, own * per_group, HEAD_SIZE), jnp.bfloat16),
            pltpu.VMEM((own, columns), jnp.int32),
            pltpu.VMEM((insts, own, columns), jnp.int32),
            pltpu.VMEM((pairs, lanes, slots * page_tok), jnp.float32),
            pltpu.VMEM((pairs, 2 * lanes, slots * page_tok), jnp.bfloat16),
            pltpu.VMEM((pairs, 2, insts, block_rows, 128), jnp.float32),
            pltpu.VMEM((pairs, devices, block_rows, 128), jnp.float32),
            pltpu.VMEM((pairs, lanes, 128), jnp.float32),
            pltpu.VMEM((groups, rows, HEAD_SIZE), jnp.float32),
            pltpu.VMEM((groups, rows, HEAD_SIZE), jnp.float32),
            pltpu.VMEM((pairs, own, per_group * HEAD_SIZE), jnp.bfloat16),
            dma((4,)), dma((2, POOL_PIECES)),
            dma((insts,)), dma((insts,)), dma((insts,)), dma((insts,)),
            dma((pairs, 2, insts)), dma((pairs, devices)),
            dma((pairs, pages)), dma((pairs, 2)), dma((pairs,)),
        ],
        compiler_params=pltpu.CompilerParams(
            collective_id=0, has_side_effects=True, vmem_limit_bytes=56 * 1024 * 1024
        ),
        cost_estimate=pl.CostEstimate(
            flops=8 * slots * page_tok * lanes * HEAD_SIZE * pairs,
            bytes_accessed=4 * slots * page_tok * depth,
            transcendentals=slots * page_tok * lanes * pairs,
        ),
        name="paged_attention",
    )(queries, fresh_key_value, lengths, block_table, key_value_pool)
    return pl.pallas_call(
        settle,
        out_shape=jax.ShapeDtypeStruct(out.shape, out.dtype),
        in_specs=[hbm],
        out_specs=hbm,
        scratch_shapes=[dma(())],
        compiler_params=pltpu.CompilerParams(vmem_limit_bytes=56 * 1024 * 1024),
        name="settle",
    )(out)


def solution(mesh):
    return jax.shard_map(
        functools.partial(shards, mesh.shape["inst"], mesh.shape["page"]),
        mesh=mesh,
        in_specs=(
            P("inst", "head"),
            P(None, "inst", "head"),
            P(None, ("inst", "page"), None, "head"),
            P("inst", None),
            P("inst"),
        ),
        out_specs=P("inst", "head"),
        check_vma=False,
    )
```

```python
import functools
import math

import jax
import jax.numpy as jnp
from jax import lax
from jax.experimental import pallas as pl
from jax.experimental.pallas import tpu as pltpu
from jax.sharding import PartitionSpec as P

HEAD_SIZE = 128
LOWEST_SCORE = -1e30
EXPONENT = math.log2(math.e) / math.sqrt(HEAD_SIZE)
BLOCK_ROWS = 16
POOL_PIECES = 4
MESH = pl.DeviceIdType.MESH


def kernel(
    insts, pages, groups,
    q_hbm, fresh_hbm, len_hbm, table_hbm, pool_hbm, out_hbm,
    q_ref, fresh_ref, len_ref, table_ref,
    keys, values, keys_by_token, values_by_token, keys_t, q_own, q_all, t_own, t_all,
    scores, weights, send, recv,
    columns_of, fresh_score, fresh_value, result,
    in_sem, pool_sem, q_send, q_recv, t_send, t_recv, x_send, x_recv, o_send, o_recv, o_own,
):
    own = q_ref.shape[0]
    heads = q_ref.shape[1] // HEAD_SIZE
    per_group = heads // groups
    pairs = groups // 2
    requests = own * insts
    columns = table_ref.shape[1]
    slots, page_tok = keys.shape[0], keys.shape[1]
    tokens = slots * page_tok
    width = requests * per_group
    lanes = 2 * width
    stat_rows = lanes // 128
    devices = insts * pages
    rows = own * per_group
    middle = pages // 2 - 1

    me_i = lax.axis_index("inst")
    me_p = lax.axis_index("page")
    me = me_i * pages + me_p
    finishes = (me_p == middle) | (me_p == middle + 1)
    side = lax.rem(me_p + pages - middle, 2)

    barrier = pltpu.get_barrier_semaphore()

    def greet(p, first):
        def one(k, carry):
            pl.semaphore_signal(
                barrier, inc=1, device_id={"inst": lax.rem(me_i + k, insts), "page": p},
                device_id_type=MESH,
            )
            return carry

        lax.fori_loop(first, insts, one, 0)

    greet(me_p, 1)

    @pl.when(finishes)
    def _():
        for k in range(1, pages):
            greet(lax.rem(me_p + k, pages), 0)

    @pl.when(jnp.logical_not(finishes))
    def _():
        for j in range(2):
            greet(middle + j, 0)

    small = [
        pltpu.make_async_copy(source, target, in_sem.at[k])
        for k, (source, target) in enumerate(
            [(q_hbm, q_ref), (len_hbm, len_ref), (table_hbm, table_ref), (fresh_hbm, fresh_ref)]
        )
    ]
    for copy in small:
        copy.start()
    piece = slots // POOL_PIECES
    pool_copies = [
        pltpu.make_async_copy(
            pool_hbm.at[kind, pl.ds(c * piece, piece)], target.at[pl.ds(c * piece, piece)],
            pool_sem.at[kind, c],
        )
        for kind, target in enumerate((keys, values))
        for c in range(POOL_PIECES)
    ]
    for copy in pool_copies:
        copy.start()
    for copy in small:
        copy.wait()

    q = q_ref[...].astype(jnp.float32)
    fresh = fresh_ref[...].astype(jnp.float32)
    grouped = []
    for g in range(groups):
        stacked = jnp.concatenate(
            [
                q[r : r + 1, (g * per_group + h) * HEAD_SIZE : (g * per_group + h + 1) * HEAD_SIZE]
                for r in range(own)
                for h in range(per_group)
            ],
            axis=0,
        )
        grouped.append(stacked)
        q_own[g] = stacked.astype(jnp.bfloat16)
    column = lax.broadcasted_iota(jnp.int32, (own, columns), 1)
    row = lax.broadcasted_iota(jnp.int32, (own, columns), 0)
    length = jnp.zeros((own, columns), jnp.int32)
    for r in range(own):
        length = jnp.where(row == r, len_ref[r], length)
    fill = jnp.clip(length - column * page_tok, 0, page_tok)
    t_own[...] = jnp.where(
        fill > 0, table_ref[...] * 1024 + (me_i * own + row) * 32 + fill, -1
    )

    @pl.when(finishes)
    def _():
        pl.semaphore_wait(barrier, devices - 1)

    @pl.when(jnp.logical_not(finishes))
    def _():
        pl.semaphore_wait(barrier, 3 * insts - 1)

    def gather_copies(k):
        to = {"inst": lax.rem(me_i + k, insts)}
        return (
            pltpu.make_async_remote_copy(
                src_ref=q_own, dst_ref=q_all.at[me_i], send_sem=q_send.at[k],
                recv_sem=q_recv.at[k], device_id=to, device_id_type=MESH,
            ),
            pltpu.make_async_remote_copy(
                src_ref=t_own, dst_ref=t_all.at[me_i], send_sem=t_send.at[k],
                recv_sem=t_recv.at[k], device_id=to, device_id_type=MESH,
            ),
        )

    for k in range(1, insts):
        for copy in gather_copies(k):
            copy.start()
    q_all[me_i] = q_own[...]
    t_all[me_i] = t_own[...]

    for g in range(groups):
        cut = slice(g * HEAD_SIZE, (g + 1) * HEAD_SIZE)
        for r in range(own):
            place = slice(r * per_group, (r + 1) * per_group)
            products = grouped[g][place] * fresh[0, r : r + 1, cut]
            score = jnp.sum(products, axis=1, keepdims=True)
            fresh_score[g, place] = jnp.broadcast_to(score, (per_group, HEAD_SIZE))
            fresh_value[g, place] = jnp.broadcast_to(fresh[1, r : r + 1, cut], (per_group, HEAD_SIZE))

    chunk = 256 // page_tok
    new = lax.broadcasted_iota(jnp.int32, (256, 256), 0)
    old = lax.broadcasted_iota(jnp.int32, (256, 256), 1)
    moves = (new // chunk == lax.rem(old, page_tok)) & (lax.rem(new, chunk) == old // page_tok)
    moves = jnp.where(moves, 1.0, 0.0).astype(jnp.bfloat16)
    for k, copy in enumerate(pool_copies):
        source, target = ((keys, keys_by_token), (values, values_by_token))[k // POOL_PIECES]
        copy.wait()
        if k == POOL_PIECES:
            for t in range(page_tok):
                keys_t[:, t * slots : (t + 1) * slots] = keys_by_token[t].T
        base = k % POOL_PIECES * piece
        for c in range(base, base + piece, chunk):
            moved = jnp.dot(
                moves, source[c : c + chunk].reshape(256, source.shape[2]),
                preferred_element_type=jnp.float32,
            )
            target[:, c : c + chunk, :] = moved.astype(jnp.bfloat16).reshape(
                page_tok, chunk, source.shape[2]
            )

    for k in range(1, insts):
        for copy in gather_copies(k):
            copy.wait()

    slot_id = lax.broadcasted_iota(jnp.int32, (slots, 128), 0) + me * slots
    code = jnp.zeros((slots, 128), jnp.int32)
    for i in range(insts):
        packed = t_all[i]
        page_id = packed >> 10
        page_code = packed & 1023
        for r in range(own):
            for b in range(0, columns, 128):
                code += jnp.where(
                    slot_id == page_id[r : r + 1, b : b + 128], page_code[r : r + 1, b : b + 128], 0
                )
    code = jnp.sum(code.astype(jnp.float32).T, axis=0, keepdims=True).astype(jnp.int32)
    slot_owner = jnp.broadcast_to(code >> 5, (BLOCK_ROWS, slots))
    slot_fill = jnp.broadcast_to(code & 31, (BLOCK_ROWS, slots))
    block_row = lax.broadcasted_iota(jnp.int32, (BLOCK_ROWS, slots), 0)
    lane = lax.broadcasted_iota(jnp.int32, (BLOCK_ROWS, 128), 1)

    def tree(join, items):
        while len(items) > 1:
            items = [join(*items[k : k + 2]) for k in range(0, len(items) - 1, 2)] + (
                items[-1:] if len(items) % 2 else []
            )
        return items[0]

    def exchange(pair, j, to_i):
        return pltpu.make_async_remote_copy(
            src_ref=send.at[pair, j, to_i], dst_ref=recv.at[pair, me],
            send_sem=x_send.at[pair, j, to_i], recv_sem=x_recv.at[pair, me],
            device_id={"inst": to_i, "page": middle + j}, device_id_type=MESH,
        )

    def all_exchanges(pair, act):
        def one(k, carry):
            for j in range(2):
                act(exchange(pair, j, lax.rem(me_i + k, insts)))
            return carry

        if insts <= 4:
            for k in range(1, insts):
                one(k, 0)
        else:
            lax.fori_loop(1, insts, one, 0)
        for j in range(2):
            @pl.when(me_p != middle + j)
            def _():
                act(exchange(pair, j, me_i))

    for pair in range(pairs):
        cut = slice(pair * 2 * HEAD_SIZE, (pair + 1) * 2 * HEAD_SIZE)
        low = q_all[:, 2 * pair].reshape(width, HEAD_SIZE)
        high = q_all[:, 2 * pair + 1].reshape(width, HEAD_SIZE)
        none = jnp.zeros_like(low)
        pair_queries = jnp.concatenate(
            [jnp.concatenate([low, none], axis=1), jnp.concatenate([none, high], axis=1)], axis=0
        )
        scores[pair] = lax.dot_general(
            pair_queries,
            keys_t[cut],
            (((1,), (0,)), ((), ())),
            preferred_element_type=jnp.float32,
        )

    for pair in range(pairs):
        cut = slice(pair * 2 * HEAD_SIZE, (pair + 1) * 2 * HEAD_SIZE)

        def weigh(block, pair=pair):
            first = block * BLOCK_ROWS
            if not isinstance(block, int):
                first = pl.multiple_of(first, BLOCK_ROWS)
            row_request = lax.rem(first + block_row, width) // per_group
            owned = (slot_owner == row_request) & (slot_fill > 0)
            masked = [
                jnp.where(
                    slot_fill > t,
                    scores[pair, pl.ds(first, BLOCK_ROWS), t * slots : (t + 1) * slots],
                    LOWEST_SCORE,
                )
                for t in range(page_tok)
            ]
            page_max = tree(jnp.maximum, masked)
            raw = [jnp.exp2((x - page_max) * EXPONENT) for x in masked]
            page_sum = tree(jnp.add, raw)
            local_max = jnp.max(
                jnp.where(owned, page_max, LOWEST_SCORE), axis=1, keepdims=True
            )
            factor = jnp.where(owned, jnp.exp2((page_max - local_max) * EXPONENT), 0.0)
            total = jnp.sum(page_sum * factor, axis=1, keepdims=True)
            for t in range(page_tok):
                scaled = raw[t].astype(jnp.bfloat16).astype(jnp.float32) * factor
                upper = scaled.astype(jnp.bfloat16)
                lower = (scaled - upper.astype(jnp.float32)).astype(jnp.bfloat16)
                at = slice(t * slots, (t + 1) * slots)
                weights[pair, pl.ds(first, BLOCK_ROWS), at] = upper
                weights[pair, pl.ds(lanes + first, BLOCK_ROWS), at] = lower
            columns_of[pair, pl.ds(first, BLOCK_ROWS)] = jnp.where(lane == 0, local_max, total)

        if lanes <= 128:
            for block in range(lanes // BLOCK_ROWS):
                weigh(block)
        else:
            lax.fori_loop(0, lanes // BLOCK_ROWS, lambda block, carry: (weigh(block), carry)[1], 0)
        both = jnp.dot(
            weights[pair], values_by_token[:, :, cut].reshape(tokens, 2 * HEAD_SIZE),
            preferred_element_type=jnp.float32,
        )
        both = both[:lanes] + both[lanes:]
        part = jnp.concatenate([both[:width, :HEAD_SIZE], both[width:, HEAD_SIZE:]], axis=0)
        stats = columns_of[pair].T
        stats = jnp.concatenate(
            [stats[k : k + 1, b * 128 : (b + 1) * 128] for k in range(2) for b in range(stat_rows)],
            axis=0,
        )
        for i in range(insts):
            for j in range(2):
                start = j * width + i * rows
                send[pair, j, i, :rows] = part[start : start + rows]
                send[pair, j, i, rows:] = stats
        all_exchanges(pair, lambda copy: copy.start())

    def result_copy(pair, k):
        at = pl.ds(pl.multiple_of((2 * pair + side) * per_group * HEAD_SIZE, 128), per_group * HEAD_SIZE)
        return pltpu.make_async_remote_copy(
            src_ref=result.at[pair], dst_ref=out_hbm.at[:, at], send_sem=o_send.at[pair, k],
            recv_sem=o_recv.at[pair, side], device_id={"page": lax.rem(me_p + k, pages)},
            device_id_type=MESH,
        )

    def own_copy(pair):
        at = pl.ds(pl.multiple_of((2 * pair + side) * per_group * HEAD_SIZE, 128), per_group * HEAD_SIZE)
        return pltpu.make_async_copy(result.at[pair], out_hbm.at[:, at], o_own.at[pair])

    @pl.when(finishes)
    def _():
        row = lax.broadcasted_iota(jnp.int32, (1, rows, 128), 1)
        lane = lax.broadcasted_iota(jnp.int32, (1, rows, 128), 2)
        place = side * width + me_i * rows + row
        for pair in range(pairs):
            recv[pair, me] = send[pair, side, me_i]

            def wait_exchange(k, carry, pair=pair):
                other = lax.rem(me + k, devices)
                pltpu.make_async_remote_copy(
                    src_ref=send.at[pair, 0, 0], dst_ref=recv.at[pair, other],
                    send_sem=x_send.at[pair, 0, 0], recv_sem=x_recv.at[pair, other],
                    device_id={"inst": lax.div(other, pages), "page": lax.rem(other, pages)},
                    device_id_type=MESH,
                ).wait_recv()
                return carry

            lax.fori_loop(1, devices, wait_exchange, 0)
            picked = []
            for kind in range(2):
                found = jnp.zeros((devices, rows, 128), jnp.float32)
                for b in range(stat_rows):
                    at = rows + kind * stat_rows + b
                    found = jnp.where(place == b * 128 + lane, recv[pair, :, at : at + 1, :], found)
                picked.append(jnp.sum(found, axis=2, keepdims=True))
            maxima, totals = picked
            own_score = fresh_score[2 * pair + side]
            top = jnp.maximum(jnp.max(maxima, axis=0), own_score)
            carried = jnp.exp2((maxima - top[None]) * EXPONENT)
            own_weight = jnp.exp2((own_score - top) * EXPONENT)
            denominator = own_weight + jnp.sum(carried * totals, axis=0)
            numerator = own_weight * fresh_value[2 * pair + side] + jnp.sum(
                carried * recv[pair, :, :rows, :], axis=0
            )
            attn = numerator / denominator
            attn = jnp.concatenate(
                [
                    jnp.concatenate(
                        [attn[r * per_group + h : r * per_group + h + 1] for h in range(per_group)],
                        axis=1,
                    )
                    for r in range(own)
                ],
                axis=0,
            )
            result[pair] = attn.astype(result.dtype)
            for k in range(1, pages):
                result_copy(pair, k).start()
            own_copy(pair).start()

    for pair in range(pairs):
        for j in range(2):
            @pl.when(me_p != middle + j)
            def _():
                at = slice(
                    (2 * pair + j) * per_group * HEAD_SIZE, (2 * pair + j + 1) * per_group * HEAD_SIZE
                )
                pltpu.make_async_remote_copy(
                    src_ref=result.at[pair], dst_ref=out_hbm.at[:, at], send_sem=o_send.at[pair, 0],
                    recv_sem=o_recv.at[pair, j], device_id={"page": middle + j},
                    device_id_type=MESH,
                ).wait_recv()

    @pl.when(finishes)
    def _():
        for pair in range(pairs):
            own_copy(pair).wait()
            for k in range(1, pages):
                result_copy(pair, k).wait_send()

    for pair in range(pairs):
        all_exchanges(pair, lambda copy: copy.wait_send())


def shards(insts, pages, queries, fresh_key_value, key_value_pool, block_table, lengths):
    own = queries.shape[0]
    slots, page_tok, depth = key_value_pool.shape[1:]
    groups = depth // HEAD_SIZE
    heads = queries.shape[1] // HEAD_SIZE
    per_group = heads // groups
    pairs = groups // 2
    columns = block_table.shape[1]
    lanes = 2 * own * insts * per_group
    devices = insts * pages
    rows = own * per_group
    block_rows = rows + 2 * lanes // 128
    hbm = pl.BlockSpec(memory_space=pl.ANY)
    dma = pltpu.SemaphoreType.DMA
    return pl.pallas_call(
        functools.partial(kernel, insts, pages, groups),
        out_shape=jax.ShapeDtypeStruct(queries.shape, jnp.bfloat16),
        in_specs=[hbm] * 5,
        out_specs=hbm,
        scratch_shapes=[
            pltpu.VMEM(queries.shape, jnp.bfloat16),
            pltpu.VMEM(fresh_key_value.shape, jnp.bfloat16),
            pltpu.SMEM(lengths.shape, jnp.int32),
            pltpu.VMEM(block_table.shape, jnp.int32),
            pltpu.VMEM((slots, page_tok, depth), jnp.bfloat16),
            pltpu.VMEM((slots, page_tok, depth), jnp.bfloat16),
            pltpu.VMEM((page_tok, slots, depth), jnp.bfloat16),
            pltpu.VMEM((page_tok, slots, depth), jnp.bfloat16),
            pltpu.VMEM((depth, slots * page_tok), jnp.bfloat16),
            pltpu.VMEM((groups, own * per_group, HEAD_SIZE), jnp.bfloat16),
            pltpu.VMEM((insts, groups, own * per_group, HEAD_SIZE), jnp.bfloat16),
            pltpu.VMEM((own, columns), jnp.int32),
            pltpu.VMEM((insts, own, columns), jnp.int32),
            pltpu.VMEM((pairs, lanes, slots * page_tok), jnp.float32),
            pltpu.VMEM((pairs, 2 * lanes, slots * page_tok), jnp.bfloat16),
            pltpu.VMEM((pairs, 2, insts, block_rows, 128), jnp.float32),
            pltpu.VMEM((pairs, devices, block_rows, 128), jnp.float32),
            pltpu.VMEM((pairs, lanes, 128), jnp.float32),
            pltpu.VMEM((groups, rows, HEAD_SIZE), jnp.float32),
            pltpu.VMEM((groups, rows, HEAD_SIZE), jnp.float32),
            pltpu.VMEM((pairs, own, per_group * HEAD_SIZE), jnp.bfloat16),
            dma((4,)), dma((2, POOL_PIECES)),
            dma((insts,)), dma((insts,)), dma((insts,)), dma((insts,)),
            dma((pairs, 2, insts)), dma((pairs, devices)),
            dma((pairs, pages)), dma((pairs, 2)), dma((pairs,)),
        ],
        compiler_params=pltpu.CompilerParams(
            collective_id=0, has_side_effects=True, vmem_limit_bytes=56 * 1024 * 1024
        ),
        cost_estimate=pl.CostEstimate(
            flops=8 * slots * page_tok * lanes * HEAD_SIZE * pairs,
            bytes_accessed=4 * slots * page_tok * depth,
            transcendentals=slots * page_tok * lanes * pairs,
        ),
        name="paged_attention",
    )(queries, fresh_key_value, lengths, block_table, key_value_pool)


def solution(mesh):
    return jax.shard_map(
        functools.partial(shards, mesh.shape["inst"], mesh.shape["page"]),
        mesh=mesh,
        in_specs=(
            P("inst", "head"),
            P(None, "inst", "head"),
            P(None, ("inst", "page"), None, "head"),
            P("inst", None),
            P("inst"),
        ),
        out_specs=P("inst", "head"),
        check_vma=False,
    )
```

```python
import functools
import math

import jax
import jax.numpy as jnp
from jax import lax
from jax.experimental import pallas as pl
from jax.experimental.pallas import tpu as pltpu
from jax.sharding import PartitionSpec as P

HEAD_SIZE = 128
LOWEST_SCORE = -1e30
EXPONENT = math.log2(math.e) / math.sqrt(HEAD_SIZE)
BLOCK_ROWS = 16
POOL_PIECES = 4
MESH = pl.DeviceIdType.MESH


def kernel(
    insts, pages, groups,
    q_hbm, fresh_hbm, len_hbm, table_hbm, pool_hbm, out_hbm,
    q_ref, fresh_ref, len_ref, table_ref,
    keys, values, keys_by_token, values_by_token, q_own, q_all, t_own, t_all,
    scores, weights, send, recv,
    columns_of, fresh_score, fresh_value, result,
    in_sem, pool_sem, q_send, q_recv, t_send, t_recv, x_send, x_recv, o_send, o_recv, o_own,
):
    own = q_ref.shape[0]
    heads = q_ref.shape[1] // HEAD_SIZE
    per_group = heads // groups
    pairs = groups // 2
    requests = own * insts
    columns = table_ref.shape[1]
    slots, page_tok = keys.shape[0], keys.shape[1]
    tokens = slots * page_tok
    width = requests * per_group
    lanes = 2 * width
    stat_rows = lanes // 128
    devices = insts * pages
    rows = own * per_group
    middle = pages // 2 - 1

    me_i = lax.axis_index("inst")
    me_p = lax.axis_index("page")
    me = me_i * pages + me_p
    finishes = (me_p == middle) | (me_p == middle + 1)
    side = lax.rem(me_p + pages - middle, 2)

    barrier = pltpu.get_barrier_semaphore()

    def greet(p, first):
        def one(k, carry):
            pl.semaphore_signal(
                barrier, inc=1, device_id={"inst": lax.rem(me_i + k, insts), "page": p},
                device_id_type=MESH,
            )
            return carry

        lax.fori_loop(first, insts, one, 0)

    greet(me_p, 1)

    @pl.when(finishes)
    def _():
        for k in range(1, pages):
            greet(lax.rem(me_p + k, pages), 0)

    @pl.when(jnp.logical_not(finishes))
    def _():
        for j in range(2):
            greet(middle + j, 0)

    small = [
        pltpu.make_async_copy(source, target, in_sem.at[k])
        for k, (source, target) in enumerate(
            [(q_hbm, q_ref), (len_hbm, len_ref), (table_hbm, table_ref), (fresh_hbm, fresh_ref)]
        )
    ]
    for copy in small:
        copy.start()
    piece = slots // POOL_PIECES
    pool_copies = [
        pltpu.make_async_copy(
            pool_hbm.at[kind, pl.ds(c * piece, piece)], target.at[pl.ds(c * piece, piece)],
            pool_sem.at[kind, c],
        )
        for kind, target in enumerate((keys, values))
        for c in range(POOL_PIECES)
    ]
    for copy in pool_copies:
        copy.start()
    for copy in small:
        copy.wait()

    q = q_ref[...].astype(jnp.float32)
    fresh = fresh_ref[...].astype(jnp.float32)
    grouped = []
    for g in range(groups):
        stacked = jnp.concatenate(
            [
                q[r : r + 1, (g * per_group + h) * HEAD_SIZE : (g * per_group + h + 1) * HEAD_SIZE]
                for r in range(own)
                for h in range(per_group)
            ],
            axis=0,
        )
        grouped.append(stacked)
        q_own[g] = stacked.astype(jnp.bfloat16)
    column = lax.broadcasted_iota(jnp.int32, (own, columns), 1)
    row = lax.broadcasted_iota(jnp.int32, (own, columns), 0)
    length = jnp.zeros((own, columns), jnp.int32)
    for r in range(own):
        length = jnp.where(row == r, len_ref[r], length)
    fill = jnp.clip(length - column * page_tok, 0, page_tok)
    t_own[...] = jnp.where(
        fill > 0, table_ref[...] * 1024 + (me_i * own + row) * 32 + fill, -1
    )

    @pl.when(finishes)
    def _():
        pl.semaphore_wait(barrier, devices - 1)

    @pl.when(jnp.logical_not(finishes))
    def _():
        pl.semaphore_wait(barrier, 3 * insts - 1)

    def gather_copies(k):
        to = {"inst": lax.rem(me_i + k, insts)}
        return (
            pltpu.make_async_remote_copy(
                src_ref=q_own, dst_ref=q_all.at[me_i], send_sem=q_send.at[k],
                recv_sem=q_recv.at[k], device_id=to, device_id_type=MESH,
            ),
            pltpu.make_async_remote_copy(
                src_ref=t_own, dst_ref=t_all.at[me_i], send_sem=t_send.at[k],
                recv_sem=t_recv.at[k], device_id=to, device_id_type=MESH,
            ),
        )

    for k in range(1, insts):
        for copy in gather_copies(k):
            copy.start()
    q_all[me_i] = q_own[...]
    t_all[me_i] = t_own[...]

    for g in range(groups):
        cut = slice(g * HEAD_SIZE, (g + 1) * HEAD_SIZE)
        for r in range(own):
            place = slice(r * per_group, (r + 1) * per_group)
            products = grouped[g][place] * fresh[0, r : r + 1, cut]
            score = jnp.sum(products, axis=1, keepdims=True)
            fresh_score[g, place] = jnp.broadcast_to(score, (per_group, HEAD_SIZE))
            fresh_value[g, place] = jnp.broadcast_to(fresh[1, r : r + 1, cut], (per_group, HEAD_SIZE))

    chunk = 256 // page_tok
    new = lax.broadcasted_iota(jnp.int32, (256, 256), 0)
    old = lax.broadcasted_iota(jnp.int32, (256, 256), 1)
    moves = (new // chunk == lax.rem(old, page_tok)) & (lax.rem(new, chunk) == old // page_tok)
    moves = jnp.where(moves, 1.0, 0.0).astype(jnp.bfloat16)
    for k, copy in enumerate(pool_copies):
        source, target = ((keys, keys_by_token), (values, values_by_token))[k // POOL_PIECES]
        copy.wait()
        base = k % POOL_PIECES * piece
        for c in range(base, base + piece, chunk):
            moved = jnp.dot(
                moves, source[c : c + chunk].reshape(256, source.shape[2]),
                preferred_element_type=jnp.float32,
            )
            target[:, c : c + chunk, :] = moved.astype(jnp.bfloat16).reshape(
                page_tok, chunk, source.shape[2]
            )

    for k in range(1, insts):
        for copy in gather_copies(k):
            copy.wait()

    slot_id = lax.broadcasted_iota(jnp.int32, (slots, 128), 0) + me * slots
    code = jnp.zeros((slots, 128), jnp.int32)
    for i in range(insts):
        packed = t_all[i]
        page_id = packed >> 10
        page_code = packed & 1023
        for r in range(own):
            for b in range(0, columns, 128):
                code += jnp.where(
                    slot_id == page_id[r : r + 1, b : b + 128], page_code[r : r + 1, b : b + 128], 0
                )
    code = jnp.sum(code.astype(jnp.float32).T, axis=0, keepdims=True).astype(jnp.int32)
    slot_owner = jnp.broadcast_to(code >> 5, (BLOCK_ROWS, slots))
    slot_fill = jnp.broadcast_to(code & 31, (BLOCK_ROWS, slots))
    block_row = lax.broadcasted_iota(jnp.int32, (BLOCK_ROWS, slots), 0)
    lane = lax.broadcasted_iota(jnp.int32, (BLOCK_ROWS, 128), 1)

    def tree(join, items):
        while len(items) > 1:
            items = [join(*items[k : k + 2]) for k in range(0, len(items) - 1, 2)] + (
                items[-1:] if len(items) % 2 else []
            )
        return items[0]

    def exchange(pair, j, to_i):
        return pltpu.make_async_remote_copy(
            src_ref=send.at[pair, j, to_i], dst_ref=recv.at[pair, me],
            send_sem=x_send.at[pair, j, to_i], recv_sem=x_recv.at[pair, me],
            device_id={"inst": to_i, "page": middle + j}, device_id_type=MESH,
        )

    def all_exchanges(pair, act):
        def one(k, carry):
            for j in range(2):
                act(exchange(pair, j, lax.rem(me_i + k, insts)))
            return carry

        if insts <= 4:
            for k in range(1, insts):
                one(k, 0)
        else:
            lax.fori_loop(1, insts, one, 0)
        for j in range(2):
            @pl.when(me_p != middle + j)
            def _():
                act(exchange(pair, j, me_i))

    for pair in range(pairs):
        cut = slice(pair * 2 * HEAD_SIZE, (pair + 1) * 2 * HEAD_SIZE)
        low = q_all[:, 2 * pair].reshape(width, HEAD_SIZE)
        high = q_all[:, 2 * pair + 1].reshape(width, HEAD_SIZE)
        none = jnp.zeros_like(low)
        pair_queries = jnp.concatenate(
            [jnp.concatenate([low, none], axis=1), jnp.concatenate([none, high], axis=1)], axis=0
        )
        scores[pair] = lax.dot_general(
            pair_queries,
            keys_by_token[:, :, cut].reshape(tokens, 2 * HEAD_SIZE),
            (((1,), (1,)), ((), ())),
            preferred_element_type=jnp.float32,
        )

    for pair in range(pairs):
        cut = slice(pair * 2 * HEAD_SIZE, (pair + 1) * 2 * HEAD_SIZE)

        def weigh(block, pair=pair):
            first = block * BLOCK_ROWS
            if not isinstance(block, int):
                first = pl.multiple_of(first, BLOCK_ROWS)
            row_request = lax.rem(first + block_row, width) // per_group
            owned = (slot_owner == row_request) & (slot_fill > 0)
            masked = [
                jnp.where(
                    slot_fill > t,
                    scores[pair, pl.ds(first, BLOCK_ROWS), t * slots : (t + 1) * slots],
                    LOWEST_SCORE,
                )
                for t in range(page_tok)
            ]
            page_max = tree(jnp.maximum, masked)
            raw = [jnp.exp2((x - page_max) * EXPONENT) for x in masked]
            page_sum = tree(jnp.add, raw)
            local_max = jnp.max(
                jnp.where(owned, page_max, LOWEST_SCORE), axis=1, keepdims=True
            )
            factor = jnp.where(owned, jnp.exp2((page_max - local_max) * EXPONENT), 0.0)
            total = jnp.sum(page_sum * factor, axis=1, keepdims=True)
            for t in range(page_tok):
                scaled = raw[t].astype(jnp.bfloat16).astype(jnp.float32) * factor
                upper = scaled.astype(jnp.bfloat16)
                lower = (scaled - upper.astype(jnp.float32)).astype(jnp.bfloat16)
                at = slice(t * slots, (t + 1) * slots)
                weights[pair, pl.ds(first, BLOCK_ROWS), at] = upper
                weights[pair, pl.ds(lanes + first, BLOCK_ROWS), at] = lower
            columns_of[pair, pl.ds(first, BLOCK_ROWS)] = jnp.where(lane == 0, local_max, total)

        if lanes <= 128:
            for block in range(lanes // BLOCK_ROWS):
                weigh(block)
        else:
            lax.fori_loop(0, lanes // BLOCK_ROWS, lambda block, carry: (weigh(block), carry)[1], 0)
        both = jnp.dot(
            weights[pair], values_by_token[:, :, cut].reshape(tokens, 2 * HEAD_SIZE),
            preferred_element_type=jnp.float32,
        )
        both = both[:lanes] + both[lanes:]
        part = jnp.concatenate([both[:width, :HEAD_SIZE], both[width:, HEAD_SIZE:]], axis=0)
        stats = columns_of[pair].T
        stats = jnp.concatenate(
            [stats[k : k + 1, b * 128 : (b + 1) * 128] for k in range(2) for b in range(stat_rows)],
            axis=0,
        )
        for i in range(insts):
            for j in range(2):
                start = j * width + i * rows
                send[pair, j, i, :rows] = part[start : start + rows]
                send[pair, j, i, rows:] = stats
        all_exchanges(pair, lambda copy: copy.start())

    def result_copy(pair, k):
        at = pl.ds(pl.multiple_of((2 * pair + side) * per_group * HEAD_SIZE, 128), per_group * HEAD_SIZE)
        return pltpu.make_async_remote_copy(
            src_ref=result.at[pair], dst_ref=out_hbm.at[:, at], send_sem=o_send.at[pair, k],
            recv_sem=o_recv.at[pair, side], device_id={"page": lax.rem(me_p + k, pages)},
            device_id_type=MESH,
        )

    def own_copy(pair):
        at = pl.ds(pl.multiple_of((2 * pair + side) * per_group * HEAD_SIZE, 128), per_group * HEAD_SIZE)
        return pltpu.make_async_copy(result.at[pair], out_hbm.at[:, at], o_own.at[pair])

    @pl.when(finishes)
    def _():
        row = lax.broadcasted_iota(jnp.int32, (1, rows, 128), 1)
        lane = lax.broadcasted_iota(jnp.int32, (1, rows, 128), 2)
        place = side * width + me_i * rows + row
        for pair in range(pairs):
            recv[pair, me] = send[pair, side, me_i]

            def wait_exchange(k, carry, pair=pair):
                other = lax.rem(me + k, devices)
                pltpu.make_async_remote_copy(
                    src_ref=send.at[pair, 0, 0], dst_ref=recv.at[pair, other],
                    send_sem=x_send.at[pair, 0, 0], recv_sem=x_recv.at[pair, other],
                    device_id={"inst": lax.div(other, pages), "page": lax.rem(other, pages)},
                    device_id_type=MESH,
                ).wait_recv()
                return carry

            lax.fori_loop(1, devices, wait_exchange, 0)
            picked = []
            for kind in range(2):
                found = jnp.zeros((devices, rows, 128), jnp.float32)
                for b in range(stat_rows):
                    at = rows + kind * stat_rows + b
                    found = jnp.where(place == b * 128 + lane, recv[pair, :, at : at + 1, :], found)
                picked.append(jnp.sum(found, axis=2, keepdims=True))
            maxima, totals = picked
            own_score = fresh_score[2 * pair + side]
            top = jnp.maximum(jnp.max(maxima, axis=0), own_score)
            carried = jnp.exp2((maxima - top[None]) * EXPONENT)
            own_weight = jnp.exp2((own_score - top) * EXPONENT)
            denominator = own_weight + jnp.sum(carried * totals, axis=0)
            numerator = own_weight * fresh_value[2 * pair + side] + jnp.sum(
                carried * recv[pair, :, :rows, :], axis=0
            )
            attn = numerator / denominator
            attn = jnp.concatenate(
                [
                    jnp.concatenate(
                        [attn[r * per_group + h : r * per_group + h + 1] for h in range(per_group)],
                        axis=1,
                    )
                    for r in range(own)
                ],
                axis=0,
            )
            result[pair] = attn.astype(result.dtype)
            for k in range(1, pages):
                result_copy(pair, k).start()
            own_copy(pair).start()

    for pair in range(pairs):
        for j in range(2):
            @pl.when(me_p != middle + j)
            def _():
                at = slice(
                    (2 * pair + j) * per_group * HEAD_SIZE, (2 * pair + j + 1) * per_group * HEAD_SIZE
                )
                pltpu.make_async_remote_copy(
                    src_ref=result.at[pair], dst_ref=out_hbm.at[:, at], send_sem=o_send.at[pair, 0],
                    recv_sem=o_recv.at[pair, j], device_id={"page": middle + j},
                    device_id_type=MESH,
                ).wait_recv()

    @pl.when(finishes)
    def _():
        for pair in range(pairs):
            own_copy(pair).wait()
            for k in range(1, pages):
                result_copy(pair, k).wait_send()

    for pair in range(pairs):
        all_exchanges(pair, lambda copy: copy.wait_send())


def shards(insts, pages, queries, fresh_key_value, key_value_pool, block_table, lengths):
    own = queries.shape[0]
    slots, page_tok, depth = key_value_pool.shape[1:]
    groups = depth // HEAD_SIZE
    heads = queries.shape[1] // HEAD_SIZE
    per_group = heads // groups
    pairs = groups // 2
    columns = block_table.shape[1]
    lanes = 2 * own * insts * per_group
    devices = insts * pages
    rows = own * per_group
    block_rows = rows + 2 * lanes // 128
    hbm = pl.BlockSpec(memory_space=pl.ANY)
    dma = pltpu.SemaphoreType.DMA
    return pl.pallas_call(
        functools.partial(kernel, insts, pages, groups),
        out_shape=jax.ShapeDtypeStruct(queries.shape, jnp.bfloat16),
        in_specs=[hbm] * 5,
        out_specs=hbm,
        scratch_shapes=[
            pltpu.VMEM(queries.shape, jnp.bfloat16),
            pltpu.VMEM(fresh_key_value.shape, jnp.bfloat16),
            pltpu.SMEM(lengths.shape, jnp.int32),
            pltpu.VMEM(block_table.shape, jnp.int32),
            pltpu.VMEM((slots, page_tok, depth), jnp.bfloat16),
            pltpu.VMEM((slots, page_tok, depth), jnp.bfloat16),
            pltpu.VMEM((page_tok, slots, depth), jnp.bfloat16),
            pltpu.VMEM((page_tok, slots, depth), jnp.bfloat16),
            pltpu.VMEM((groups, own * per_group, HEAD_SIZE), jnp.bfloat16),
            pltpu.VMEM((insts, groups, own * per_group, HEAD_SIZE), jnp.bfloat16),
            pltpu.VMEM((own, columns), jnp.int32),
            pltpu.VMEM((insts, own, columns), jnp.int32),
            pltpu.VMEM((pairs, lanes, slots * page_tok), jnp.float32),
            pltpu.VMEM((pairs, 2 * lanes, slots * page_tok), jnp.bfloat16),
            pltpu.VMEM((pairs, 2, insts, block_rows, 128), jnp.float32),
            pltpu.VMEM((pairs, devices, block_rows, 128), jnp.float32),
            pltpu.VMEM((pairs, lanes, 128), jnp.float32),
            pltpu.VMEM((groups, rows, HEAD_SIZE), jnp.float32),
            pltpu.VMEM((groups, rows, HEAD_SIZE), jnp.float32),
            pltpu.VMEM((pairs, own, per_group * HEAD_SIZE), jnp.bfloat16),
            dma((4,)), dma((2, POOL_PIECES)),
            dma((insts,)), dma((insts,)), dma((insts,)), dma((insts,)),
            dma((pairs, 2, insts)), dma((pairs, devices)),
            dma((pairs, pages)), dma((pairs, 2)), dma((pairs,)),
        ],
        compiler_params=pltpu.CompilerParams(
            collective_id=0, has_side_effects=True, vmem_limit_bytes=56 * 1024 * 1024
        ),
        cost_estimate=pl.CostEstimate(
            flops=8 * slots * page_tok * lanes * HEAD_SIZE * pairs,
            bytes_accessed=4 * slots * page_tok * depth,
            transcendentals=slots * page_tok * lanes * pairs,
        ),
        name="paged_attention",
    )(queries, fresh_key_value, lengths, block_table, key_value_pool)


def solution(mesh):
    return jax.shard_map(
        functools.partial(shards, mesh.shape["inst"], mesh.shape["page"]),
        mesh=mesh,
        in_specs=(
            P("inst", "head"),
            P(None, "inst", "head"),
            P(None, ("inst", "page"), None, "head"),
            P("inst", None),
            P("inst"),
        ),
        out_specs=P("inst", "head"),
        check_vma=False,
    )
```
